32 devices in a mesh: grp: 2 (over x), ta: 4 (over y, core), xyz: 4 (over z).
Axes of the slice: x: 2, y: 2, z: 4, core: 2. Of those that a mesh axis runs over, the one named last changes fastest.
Arguments:
- links: float32 [4, 3, 3, 2, 8, 4, 256], P(None, None, None, None, ('grp', 'ta'), 'xyz'), may hold values from -1 to 1, as said below
- momenta: float32 [4, 3, 3, 2, 8, 4, 256], P(None, None, None, None, ('grp', 'ta'), 'xyz'), may hold values from -11 to 11, as said below
- vectors: float32 [16, 3, 2, 2, 4, 4, 256], P('grp', None, None, None, 'ta', 'xyz'), may hold values from -6 to 6
- coefficients: float32 [4], replicated, may hold values from -1 to 1
Outputs:
- new_links: float32 [4, 3, 3, 2, 8, 4, 256], P(None, None, None, None, ('grp', 'ta'), 'xyz')
- new_momenta: float32 [4, 3, 3, 2, 8, 4, 256], P(None, None, None, None, ('grp', 'ta'), 'xyz')
- filtered: float32 [16, 3, 2, 2, 4, 4, 256], P('grp', None, None, None, 'ta', 'xyz')
The draws below stay inside these ranges and needn't reach their ends.
Inputs may be any that keep to these rules, and one draw needn't show every extreme that they name: `links`: every 3 x 3 link matrix is special unitary up to rounding. `momenta`: every 3 x 3 momentum matrix is anti-Hermitian and traceless: an entry below the diagonal has exactly the negated real part and the same imaginary part as its mirror above, the diagonal has zero real parts.
All inputs are finite; a program needn't handle non-finite values.
Results may differ from the reference program's by a relative error of at most 0.0001.
Values sent between devices are 32-bit elements; how exact they have to be, the bound alone decides.
A program may use at most 64 MiB of HBM per device.

```python
import jax
import jax.numpy as jnp
from jax import lax

NV = 16
NY = 8
NZ = 32
NSTEP = 2
NCHEB = 3
NT = 8
NHALF = 4
NX = 4


def conjugate_inner(left_side, right_side):
    real_part = jnp.sum(left_side[:, :, 0] * right_side[:, :, 0] + left_side[:, :, 1] * right_side[:, :, 1], axis=1)
    imag_part = jnp.sum(left_side[:, :, 0] * right_side[:, :, 1] - left_side[:, :, 1] * right_side[:, :, 0], axis=1)
    return (real_part, imag_part)


def draw_links(key, part):
    shape_sites = (NT, NX, NY * NZ)
    sample = jax.random.normal(key, (2, 4, 3, 2) + shape_sites, jnp.float32)
    row_one = sample[0]
    row_one = row_one / jnp.sqrt(jnp.sum(row_one * row_one, axis=(1, 2)))[:, None, None]
    correlation_re, correlation_im = conjugate_inner(row_one, sample[1])
    second_re = sample[1][:, :, 0] - (correlation_re[:, None] * row_one[:, :, 0] - correlation_im[:, None] * row_one[:, :, 1])
    second_im = sample[1][:, :, 1] - (correlation_re[:, None] * row_one[:, :, 1] + correlation_im[:, None] * row_one[:, :, 0])
    row_two = jnp.stack([second_re, second_im], axis=2)
    row_two = row_two / jnp.sqrt(jnp.sum(row_two * row_two, axis=(1, 2)))[:, None, None]
    one_re = row_one[:, :, 0]
    one_im = row_one[:, :, 1]
    two_re = row_two[:, :, 0]
    two_im = row_two[:, :, 1]
    pieces = []
    for colour in range(3):
        second_col = (colour + 1) % 3
        third_col = (colour + 2) % 3
        cross_re = one_re[:, second_col] * two_re[:, third_col] - one_im[:, second_col] * two_im[:, third_col] - (one_re[:, third_col] * two_re[:, second_col] - one_im[:, third_col] * two_im[:, second_col])
        cross_im = one_re[:, second_col] * two_im[:, third_col] + one_im[:, second_col] * two_re[:, third_col] - (one_re[:, third_col] * two_im[:, second_col] + one_im[:, third_col] * two_re[:, second_col])
        pieces.append(jnp.stack([cross_re, -cross_im], axis=1))
    row_three = jnp.stack(pieces, axis=1)
    generic = jnp.stack([row_one, row_two, row_three], axis=1)
    plant_key = jax.random.fold_in(key, 7)
    phase_key = jax.random.fold_in(key, 11)
    planted = jax.random.randint(plant_key, (4,) + shape_sites, 0, 16) == 0
    phases = jax.random.uniform(phase_key, (2, 4) + shape_sites, jnp.float32, -jnp.pi, jnp.pi)
    angles = jnp.stack([phases[0], phases[1], -(phases[0] + phases[1])], axis=1)
    unit_eye = jnp.eye(3, dtype=jnp.float32).reshape(1, 3, 3, 1, 1, 1)
    phase_re = unit_eye * jnp.cos(angles)[:, :, None]
    phase_im = unit_eye * jnp.sin(angles)[:, :, None]
    phase_matrix = jnp.stack([phase_re, phase_im], axis=3)
    return jnp.where(planted[:, None, None, None], phase_matrix, generic)


def draw_momenta(key, part):
    shape_all = (4, 3, 3, 2, NT, NX, NY * NZ)
    sample = jnp.clip(jax.random.normal(key, shape_all, jnp.float32), -4.0, 4.0)
    real_part = (sample[:, :, :, 0] - jnp.swapaxes(sample[:, :, :, 0], 1, 2)) * 0.5
    imag_part = (sample[:, :, :, 1] + jnp.swapaxes(sample[:, :, :, 1], 1, 2)) * 0.5
    diagonal = (imag_part[:, 0, 0] + imag_part[:, 1, 1] + imag_part[:, 2, 2]) / 3.0
    unit_eye = jnp.eye(3, dtype=jnp.float32).reshape(1, 3, 3, 1, 1, 1)
    imag_part = imag_part - unit_eye * diagonal[:, None, None]
    return jnp.stack([real_part, imag_part], axis=3)


def steps_of(own_key, extent, split, smallest, top_value):
    def one(position, parts):
        steps = jax.random.uniform(jax.random.fold_in(jax.random.fold_in(own_key, 6), position), (parts,), jnp.float32, smallest / len(split), top_value / len(split))
        return jnp.repeat(jnp.exp(steps), extent[position] // parts).reshape((-1,) + (1,) * (len(extent) - position - 1))

    gain = one(*split[0])
    for cut in split[1:]:
        gain = gain * one(*cut)
    return gain


def centred(own_key, shape, scale, bound, cuts=(), held_as=jnp.bfloat16):
    factor_of = steps_of(own_key, shape, cuts, -0.22, 0.18) if cuts else 1.0
    drawn = jax.random.normal(own_key, shape, jnp.float32) * scale * factor_of
    return jnp.minimum(jnp.maximum(drawn, -bound), bound).astype(held_as)


def setup_inputs(seed: int = 0) -> dict:
    splits = jax.random.split(jax.random.key(seed), 5)
    return {
        "links": draw_links(jax.random.fold_in(splits[4], 71), 0),
        "momenta": draw_momenta(jax.random.fold_in(splits[4], 71), 0),
        "vectors": centred(splits[2], (NV, 3, 2, 2, NHALF, NX, NY * NZ), 1.0, 6.0, ((0, 2), (4, 4), (5, 4)), jnp.float32),
        "coefficients": jnp.clip(jax.random.uniform(splits[3], (NCHEB + 1,), jnp.float32, -1.0, 1.0), -1.0, 1.0),
    }


coupling = 5.7
time_step = 0.1
taylor_degree = 6


def matrix_product(left_side, right_side):
    left_re = left_side[:, :, 0]
    left_im = left_side[:, :, 1]
    right_re = right_side[:, :, 0]
    right_im = right_side[:, :, 1]
    real_part = jnp.sum(left_re[:, :, None] * right_re[None] - left_im[:, :, None] * right_im[None], axis=1)
    imag_part = jnp.sum(left_re[:, :, None] * right_im[None] + left_im[:, :, None] * right_re[None], axis=1)
    return jnp.stack([real_part, imag_part], axis=2)


def hermitian_transpose(color_matrix):
    return jnp.stack([jnp.swapaxes(color_matrix[:, :, 0], 0, 1), -jnp.swapaxes(color_matrix[:, :, 1], 0, 1)], axis=2)


def identity_like(color_matrix):
    unit_eye = jnp.eye(3, dtype=jnp.float32).reshape((3, 3) + (1,) * (color_matrix.ndim - 3))
    real_part = jnp.broadcast_to(unit_eye, color_matrix[:, :, 0].shape)
    return jnp.stack([real_part, jnp.zeros_like(real_part)], axis=2)


def traceless_part(color_matrix):
    skew_part = (color_matrix - hermitian_transpose(color_matrix)) * 0.5
    trace_im = (skew_part[0, 0, 1] + skew_part[1, 1, 1] + skew_part[2, 2, 1]) / 3.0
    unit_eye = jnp.eye(3, dtype=jnp.float32).reshape((3, 3) + (1,) * trace_im.ndim)
    return jnp.stack([skew_part[:, :, 0], skew_part[:, :, 1] - unit_eye * trace_im], axis=2)


def taylor_exp(generator):
    identity = identity_like(generator)
    result = identity
    for degree in range(taylor_degree, 0, -1):
        result = identity + matrix_product(generator, result) / degree
    return result


def shift_lattice(entry_values, direction, amount):
    return jnp.roll(entry_values, -amount, axis=entry_values.ndim - 4 + direction)


def gauge_force(lattice):
    forces = []
    for direction in range(4):
        staple = jnp.zeros_like(lattice[0])
        for across in range(4):
            if across == direction:
                continue
            up_part = matrix_product(matrix_product(shift_lattice(lattice[across], direction, 1), hermitian_transpose(shift_lattice(lattice[direction], across, 1))), hermitian_transpose(lattice[across]))
            low_part = matrix_product(matrix_product(hermitian_transpose(shift_lattice(shift_lattice(lattice[across], direction, 1), across, -1)), hermitian_transpose(shift_lattice(lattice[direction], across, -1))), shift_lattice(lattice[across], across, -1))
            staple = staple + up_part
            staple = staple + low_part
        forces.append((coupling / 3.0) * traceless_part(matrix_product(lattice[direction], staple)))
    return jnp.stack(forces)


def multiply_by_matrix(color_matrix, entry_values):
    matrix_re = color_matrix[:, :, 0][None]
    matrix_im = color_matrix[:, :, 1][None]
    values_re = entry_values[:, :, 0][:, None]
    values_im = entry_values[:, :, 1][:, None]
    real_part = jnp.sum(matrix_re * values_re - matrix_im * values_im, axis=2)
    imag_part = jnp.sum(matrix_re * values_im + matrix_im * values_re, axis=2)
    return jnp.stack([real_part, imag_part], axis=2)


def hopping(spatial, entry_values):
    summand_terms = []
    for lattice_direction in range(3):
        color_matrix = spatial[lattice_direction]
        summand_terms.append(multiply_by_matrix(color_matrix, shift_lattice(entry_values, lattice_direction + 1, 1)))
        summand_terms.append(multiply_by_matrix(hermitian_transpose(shift_lattice(color_matrix, lattice_direction + 1, -1)), shift_lattice(entry_values, lattice_direction + 1, -1)))
    running_total = summand_terms[0]
    for summand_term in summand_terms[1:]:
        running_total = running_total + summand_term
    return running_total


def chebyshev(spatial, entry_values, coefficients):
    previous = entry_values
    current = hopping(spatial, entry_values) * (-1.0 / 6.0)
    result = coefficients[0] * previous
    result = result + coefficients[1] * current
    for degree in range(2, NCHEB + 1):
        following = 2.0 * (hopping(spatial, current) * (-1.0 / 6.0)) - previous
        result = result + coefficients[degree] * following
        previous = current
        current = following
    return result


def reference(links, momenta, vectors, coefficients):
    shape_links = links.shape
    batched_exp = jax.vmap(taylor_exp)
    batched_product = jax.vmap(matrix_product)
    lattice = links.reshape(4, 3, 3, 2, NT, NX, NY, NZ)
    moment = momenta.reshape(4, 3, 3, 2, NT, NX, NY, NZ)
    force_field = gauge_force(lattice)
    moment = moment - (0.5 * time_step) * force_field
    for counter in range(NSTEP):
        lattice = batched_product(batched_exp(time_step * moment), lattice)
        force_field = gauge_force(lattice)
        if counter + 1 < NSTEP:
            moment = moment - time_step * force_field
        else:
            moment = moment - (0.5 * time_step) * force_field
    spatial = [lattice[1], lattice[2], lattice[3]]
    fields = vectors.reshape(NV, 3, 2, NT, NX, NY, NZ)

    def filter_one(entry_values):
        return chebyshev(spatial, entry_values[None], coefficients)[0]

    filtered = lax.map(filter_one, fields)
    return lattice.reshape(shape_links), moment.reshape(shape_links), filtered.reshape(vectors.shape)
```

```python
import functools

import jax
import jax.numpy as jnp
from jax import lax
from jax.experimental import pallas as pl
from jax.experimental.pallas import tpu as pltpu
from jax.sharding import PartitionSpec as P

NZ = 32
NSTEP = 2
NCHEB = 3

coupling = 5.7
time_step = 0.1

LANES = 128
ROWS = 8
F32 = jnp.float32
UPPER = ((0, 1), (0, 2), (1, 2))


def iota(shape, dim):
    return lax.broadcasted_iota(jnp.int32, shape, len(shape) + dim)


def row_roll(values, count):
    count = count % 4
    if count == 0:
        return values
    return pltpu.roll(values, ROWS - 2 * count, axis=values.ndim - 2)


def swap_halves(values):
    axis = values.ndim - 2
    return jnp.where(
        iota(values.shape, -2) % 2 == 0,
        pltpu.roll(values, ROWS - 1, axis=axis),
        pltpu.roll(values, 1, axis=axis),
    )


def roll_y(values, amount):
    lane = iota(values.shape, -1)
    axis = values.ndim - 1
    if amount == 1:
        moved = pltpu.roll(values, LANES - NZ, axis=axis)
        return jnp.where(lane < LANES - NZ, moved, swap_halves(moved))
    moved = pltpu.roll(values, NZ, axis=axis)
    return jnp.where(lane >= NZ, moved, swap_halves(moved))


def roll_z(values, amount):
    position = iota(values.shape, -1) % NZ
    axis = values.ndim - 1
    if amount == 1:
        return jnp.where(
            position == NZ - 1,
            pltpu.roll(values, NZ - 1, axis=axis),
            pltpu.roll(values, LANES - 1, axis=axis),
        )
    return jnp.where(
        position == 0,
        pltpu.roll(values, LANES - NZ + 1, axis=axis),
        pltpu.roll(values, 1, axis=axis),
    )


def by_pair(choices):
    row = iota(choices[0].shape, -2)
    return jnp.where(
        row < 4,
        jnp.where(row < 2, choices[0], choices[1]),
        jnp.where(row < 6, choices[2], choices[3]),
    )


def product(left, right, left_h=False, right_h=False):
    real = imag = None
    for c in range(3):
        lr, li = (left[0, c], left[1, c]) if left_h else (left[0, :, c], left[1, :, c])
        rr, ri = (right[0, :, c], right[1, :, c]) if right_h else (right[0, c], right[1, c])
        lr, li, rr, ri = lr[:, None], li[:, None], rr[None], ri[None]
        both = lr * rr
        cross = li * ri
        first = lr * ri
        second = li * rr
        re = both + cross if left_h != right_h else both - cross
        if left_h and right_h:
            im = -first - second
        elif left_h:
            im = first - second
        elif right_h:
            im = second - first
        else:
            im = first + second
        real = re if real is None else real + re
        imag = im if imag is None else imag + im
    return jnp.stack([real, imag])


def traceless_part(m):
    parts = [0.5 * (m[0, i, j] - m[0, j, i]) for i, j in UPPER]
    parts += [0.5 * (m[1, i, j] + m[1, j, i]) for i, j in UPPER]
    trace = (m[1, 0, 0] + m[1, 1, 1] + m[1, 2, 2]) * (1.0 / 3.0)
    parts += [m[1, i, i] - trace for i in range(3)]
    return jnp.stack(parts)


def gauge_force(own, plus_t, plus_x, minus_t, minus_x, corner):
    ahead = [plus_t, plus_x, roll_y(own, 1), roll_z(own, 1)]
    behind = [minus_t, minus_x, roll_y(own, -1), roll_z(own, -1)]

    def slanted(arrays, k):
        return by_pair([arrays[(nu - k) % 4] for nu in range(4)])

    diagonal = slanted(behind, 0)
    turned = [
        by_pair([corner, corner, roll_y(plus_t, -1), roll_z(plus_t, -1)]),
        by_pair([corner, corner, roll_y(plus_x, -1), roll_z(plus_x, -1)]),
        roll_y(diagonal, 1),
        roll_z(diagonal, 1),
    ]
    staple = None
    for k in (1, 2, 3):
        up = product(
            product(row_roll(slanted(ahead, k), k), slanted(ahead, 4 - k), right_h=True),
            row_roll(own, k),
            right_h=True,
        )
        low = product(
            product(row_roll(slanted(turned, k), k), slanted(behind, 4 - k), True, True),
            row_roll(diagonal, k),
        )
        staple = up + low if staple is None else staple + up + low
    return (coupling / 3.0) * traceless_part(product(own, staple))


def third_row(two):
    re, im = [], []
    for colour in range(3):
        b, c = (colour + 1) % 3, (colour + 2) % 3
        ar, ai, dr, di = two[0, 0, b], two[1, 0, b], two[0, 1, c], two[1, 1, c]
        er, ei, fr, fi = two[0, 0, c], two[1, 0, c], two[0, 1, b], two[1, 1, b]
        re.append(ar * dr - ai * di - (er * fr - ei * fi))
        im.append(-(ar * di + ai * dr - (er * fi + ei * fr)))
    return jnp.stack([jnp.stack(re), jnp.stack(im)])


def evolve(moment, own):
    a = time_step * moment
    x01, x02, x12 = a[3], a[4], a[5]
    y01, y02, y12 = -a[0], -a[1], -a[2]
    h0, h1, h2 = a[6], a[7], a[8]
    n01 = x01 * x01 + y01 * y01
    n02 = x02 * x02 + y02 * y02
    n12 = x12 * x12 + y12 * y12
    g0 = h0 * h0 + n01 + n02
    g1 = h1 * h1 + n01 + n12
    g2 = h2 * h2 + n02 + n12
    u01 = (h0 + h1) * x01 + (x02 * x12 + y02 * y12)
    v01 = (h0 + h1) * y01 + (y02 * x12 - x02 * y12)
    p02 = x01 * x12 - y01 * y12
    q02 = x01 * y12 + y01 * x12
    u02 = (h0 + h2) * x02 + p02
    v02 = (h0 + h2) * y02 + q02
    u12 = (h1 + h2) * x12 + (x01 * x02 + y01 * y02)
    v12 = (h1 + h2) * y12 + (x01 * y02 - y01 * x02)
    s = 0.5 * (g0 + g1 + g2)
    d = (
        h0 * h1 * h2
        + 2.0 * (p02 * x02 + q02 * y02)
        - h0 * n12
        - h1 * n02
        - h2 * n01
    )
    c0r = 1.0 - d * d * (1.0 / 720.0)
    c0i = d * (s * (1.0 / 120.0) - 1.0 / 6.0)
    c1r = d * (1.0 / 24.0 - s * (1.0 / 360.0))
    c1i = 1.0 + s * (s * (1.0 / 120.0) - 1.0 / 6.0)
    c2r = s * (1.0 / 24.0 - s * (1.0 / 720.0)) - 0.5
    c2i = d * (1.0 / 120.0)
    re = [[None] * 3 for _ in range(3)]
    im = [[None] * 3 for _ in range(3)]
    for i, (h, g) in enumerate(((h0, g0), (h1, g1), (h2, g2))):
        re[i][i] = c0r + c1r * h + c2r * g
        im[i][i] = c0i + c1i * h + c2i * g
    for (i, j), x, y, u, v in (
        ((0, 1), x01, y01, u01, v01),
        ((0, 2), x02, y02, u02, v02),
        ((1, 2), x12, y12, u12, v12),
    ):
        rx = c1r * x + c2r * u
        iy = c1i * y + c2i * v
        ix = c1i * x + c2i * u
        ry = c1r * y + c2r * v
        re[i][j], re[j][i] = rx - iy, rx + iy
        im[i][j], im[j][i] = ix + ry, ix - ry
    e = jnp.stack([jnp.stack([jnp.stack(r) for r in re]), jnp.stack([jnp.stack(r) for r in im])])
    return product(e, own)


def spread(values, pair):
    return by_pair([row_roll(values, pair - p) for p in range(4)])


def matvec(matrix, v, herm=False):
    real = imag = None
    for c in range(3):
        mr, mi = (matrix[0, c], matrix[1, c]) if herm else (matrix[0, :, c], matrix[1, :, c])
        vr, vi = v[0, c][None], v[1, c][None]
        if herm:
            re = mr * vr + mi * vi
            im = mr * vi - mi * vr
        else:
            re = mr * vr - mi * vi
            im = mr * vi + mi * vr
        real = re if real is None else real + re
        imag = im if imag is None else imag + im
    return jnp.stack([real, imag])


def kernel(
    sizes,
    coef,
    u_ref,
    p_ref,
    mine_ref,
    give_ref,
    u_out,
    p_out,
    keep_out,
    back_out,
    state,
    pair_u,
    got_u,
    got_pair_u,
    send_p,
    pair_p,
    got_p,
    got_pair_p,
    hop_links,
    fields,
    got_fields,
    total,
    partial,
    got_back,
    send_sem,
    recv_sem,
):
    n_grp, n_ta, n_x = sizes
    grp, ta, x = lax.axis_index("grp"), lax.axis_index("ta"), lax.axis_index("xyz")
    n_t = n_grp * n_ta
    t = grp * n_ta + ta

    def device(dt, dx):
        tt = lax.rem(t + dt + n_t, n_t)
        return (tt // n_ta, lax.rem(tt, n_ta), lax.rem(x + dx + n_x, n_x))

    partner = (lax.rem(grp + 1, n_grp), ta, x)
    whole_to = [device(-1, 0), device(0, -1), device(1, 0), device(0, 1)]
    pair_to = [device(1, -1), device(-1, 1)]
    peers = whole_to + pair_to + [partner]
    barrier = pltpu.get_barrier_semaphore()
    for peer in peers:
        pl.semaphore_signal(
            barrier, inc=1, device_id=peer, device_id_type=pl.DeviceIdType.MESH
        )

    counter = [0]

    def copy(src, dst, to):
        n = counter[0]
        counter[0] += 1
        made = pltpu.make_async_remote_copy(
            src_ref=src,
            dst_ref=dst,
            send_sem=send_sem.at[n],
            recv_sem=recv_sem.at[n],
            device_id=to,
            device_id_type=pl.DeviceIdType.MESH,
        )
        made.start()
        return made

    pending = []

    pair_u[0] = u_ref[:, 0:2, :, 0:2, :]
    pair_u[1] = u_ref[:, 0:2, :, 2:4, :]
    state[0] = u_ref[...]
    pl.semaphore_wait(barrier, len(peers))

    first = [copy(u_ref.at[:, 0:2], got_u.at[i], whole_to[i]) for i in (1, 3, 0, 2)]
    first += [copy(pair_u.at[i], got_pair_u.at[i], pair_to[i]) for i in range(2)]
    give = copy(give_ref, fields.at[0, 2:4], partner)
    fields[0, 0:2] = mine_ref[...]
    pending += first + [give]
    for made in first:
        made.wait_recv()
    for i in range(4):
        state[i + 1, :, 0:2] = got_u[i]
        state[i + 1, :, 2] = third_row(got_u[i])
    low, high = got_pair_u[0], got_pair_u[1]
    both = jnp.concatenate([low, high, high, high], axis=3)
    state[5, :, 0:2] = both
    state[5, :, 2] = third_row(both)

    def force():
        return gauge_force(*[state[i] for i in range(6)])

    def send_moment(r, moment):
        send_p[r] = moment
        pair_p[r, 0] = moment[:, 0:2, :]
        pair_p[r, 1] = moment[:, 2:4, :]
        made = [copy(send_p.at[r], got_p.at[r, i], whole_to[i]) for i in (1, 3, 0, 2)]
        made += [copy(pair_p.at[r, i], got_pair_p.at[r, i], pair_to[i]) for i in range(2)]
        return made

    def send_fields(r):
        return [
            copy(fields.at[r], got_fields.at[r, 0], whole_to[1]),
            copy(fields.at[r], got_fields.at[r, 1], whole_to[3]),
        ]

    halo = None
    moment = p_ref[...] - (0.5 * time_step) * force()
    for r in range(NSTEP):
        made = send_moment(r, moment)
        pending += made
        if r == 0:
            give.wait_recv()
            halo = send_fields(0)
            pending += halo
        state[0] = evolve(moment, state[0])
        for one in made:
            one.wait_recv()

        @pl.loop(0, 4)
        def _(i):
            state[i + 1] = evolve(got_p[r, i], state[i + 1])

        low, high = got_pair_p[r, 0], got_pair_p[r, 1]
        state[5] = evolve(jnp.concatenate([low, high, high, high], axis=1), state[5])
        if r + 1 < NSTEP:
            moment = moment - time_step * force()

    own = state[0]
    u_out[...] = own
    backs = [state[4], roll_y(own, -1), roll_z(own, -1)]
    for i in range(3):
        hop_links[2 * i] = spread(own, i + 1)
        hop_links[2 * i + 1] = spread(backs[i], i + 1)

    def local_terms(k):
        @pl.loop(0, 4)
        def _(g):
            v = fields[k, g]
            acc = matvec(hop_links[2], roll_y(v, 1))
            acc = acc + matvec(hop_links[3], roll_y(v, -1), True)
            acc = acc + matvec(hop_links[4], roll_z(v, 1))
            partial[g] = acc + matvec(hop_links[5], roll_z(v, -1), True)

    def finish(k):
        scale = -1.0 / 6.0

        @pl.loop(0, 4)
        def _(g):
            acc = partial[g] + matvec(hop_links[0], got_fields[k, 0, g])
            acc = (acc + matvec(hop_links[1], got_fields[k, 1, g], True)) * scale
            if k == 0:
                fields[1, g] = acc
                total[g] = coef[0] * fields[0, g] + coef[1] * acc
            else:
                following = 2.0 * acc - fields[k - 1, g]
                if k + 1 < NCHEB:
                    fields[k + 1, g] = following
                total[g] = total[g] + coef[k + 1] * following

    for k in range(NCHEB):
        if k:
            halo = send_fields(k)
            pending += halo
        if k == 1:
            p_out[...] = moment - (0.5 * time_step) * force()
        local_terms(k)
        for one in halo:
            one.wait_recv()
        finish(k)
    back = copy(total.at[2:4], got_back, partner)
    keep_out[...] = total[0:2]
    back.wait_recv()
    back_out[...] = got_back[...]
    for one in pending + [back]:
        one.wait_send()


def body(sizes, links, momenta, vectors, coefficients):
    n_vec = vectors.shape[0]
    tiles = n_vec * 2 // ROWS
    u = links.reshape(4, 3, 3, 2, 2, LANES).transpose(3, 1, 2, 0, 4, 5)
    u = u.reshape(2, 3, 3, ROWS, LANES)
    m = momenta.reshape(4, 3, 3, 2, 2, LANES)
    p = jnp.stack(
        [m[:, i, j, 0] for i, j in UPPER]
        + [m[:, i, j, 1] for i, j in UPPER]
        + [m[:, i, i, 1] for i in range(3)]
    ).reshape(9, ROWS, LANES)
    v = vectors.reshape(tiles, 4, 3, 2, 2, 2, LANES).transpose(4, 0, 3, 2, 1, 5, 6)
    v = v.reshape(2, tiles, 2, 3, ROWS, LANES)
    low_half = lax.axis_index("grp") == 0
    mine = jnp.where(low_half, v[0], v[1])
    give = jnp.where(low_half, v[1], v[0])

    groups = 2 * tiles
    copies = 6 + 6 * NSTEP + 1 + 2 * NCHEB + 1
    vmem = pl.BlockSpec(memory_space=pltpu.VMEM)
    tile = (ROWS, LANES)
    new_u, new_p, keep, back = pl.pallas_call(
        functools.partial(kernel, sizes),
        out_shape=(
            jax.ShapeDtypeStruct((2, 3, 3) + tile, F32),
            jax.ShapeDtypeStruct((9,) + tile, F32),
            jax.ShapeDtypeStruct((tiles, 2, 3) + tile, F32),
            jax.ShapeDtypeStruct((tiles, 2, 3) + tile, F32),
        ),
        in_specs=[pl.BlockSpec(memory_space=pltpu.SMEM)] + [vmem] * 4,
        out_specs=(vmem,) * 4,
        scratch_shapes=[
            pltpu.VMEM((6, 2, 3, 3) + tile, F32),
            pltpu.VMEM((2, 2, 2, 3, 2, LANES), F32),
            pltpu.VMEM((4, 2, 2, 3) + tile, F32),
            pltpu.VMEM((2, 2, 2, 3, 2, LANES), F32),
            pltpu.VMEM((NSTEP, 9) + tile, F32),
            pltpu.VMEM((NSTEP, 2, 9, 2, LANES), F32),
            pltpu.VMEM((NSTEP, 4, 9) + tile, F32),
            pltpu.VMEM((NSTEP, 2, 9, 2, LANES), F32),
            pltpu.VMEM((6, 2, 3, 3) + tile, F32),
            pltpu.VMEM((NCHEB, groups, 2, 3) + tile, F32),
            pltpu.VMEM((NCHEB, 2, groups, 2, 3) + tile, F32),
            pltpu.VMEM((groups, 2, 3) + tile, F32),
            pltpu.VMEM((groups, 2, 3) + tile, F32),
            pltpu.VMEM((tiles, 2, 3) + tile, F32),
            pltpu.SemaphoreType.DMA((copies,)),
            pltpu.SemaphoreType.DMA((copies,)),
        ],
        compiler_params=pltpu.CompilerParams(
            collective_id=0, has_side_effects=True, vmem_limit_bytes=32 * 1024 * 1024
        ),
    )(coefficients, u, p, mine, give)

    new_links = new_u.reshape(2, 3, 3, 4, 2, LANES).transpose(3, 1, 2, 0, 4, 5)
    new_links = new_links.reshape(links.shape)
    q = new_p.reshape(9, 4, 2 * LANES)
    zero = jnp.zeros_like(q[0])
    where = {pair: n for n, pair in enumerate(UPPER)}
    entries = []
    for i in range(3):
        for j in range(3):
            if i == j:
                entries += [zero, q[6 + i]]
            elif i < j:
                entries += [q[where[i, j]], q[3 + where[i, j]]]
            else:
                entries += [-q[where[j, i]], q[3 + where[j, i]]]
    new_momenta = jnp.stack(entries, axis=1).reshape(momenta.shape)
    out = jnp.stack([jnp.where(low_half, keep, back), jnp.where(low_half, back, keep)])
    out = out.reshape(2, tiles, 2, 3, 4, 2, LANES).transpose(1, 4, 3, 2, 0, 5, 6)
    return new_links, new_momenta, out.reshape(vectors.shape)


def solution(mesh):
    sizes = (mesh.shape["grp"], mesh.shape["ta"], mesh.shape["xyz"])
    link_spec = P(None, None, None, None, ("grp", "ta"), "xyz", None)
    vector_spec = P("grp", None, None, None, "ta", "xyz", None)
    return jax.shard_map(
        functools.partial(body, sizes),
        mesh=mesh,
        in_specs=(link_spec, link_spec, vector_spec, P()),
        out_specs=(link_spec, link_spec, vector_spec),
        check_vma=False,
    )
```

```python
import functools

import jax
import jax.numpy as jnp
from jax import lax
from jax.experimental import pallas as pl
from jax.experimental.pallas import tpu as pltpu
from jax.sharding import PartitionSpec as P

NZ = 32
NSTEP = 2
NCHEB = 3

coupling = 5.7
time_step = 0.1

LANES = 128
ROWS = 8
F32 = jnp.float32
UPPER = ((0, 1), (0, 2), (1, 2))


def iota(shape, dim):
    return lax.broadcasted_iota(jnp.int32, shape, len(shape) + dim)


def row_roll(values, count):
    count = count % 4
    if count == 0:
        return values
    return pltpu.roll(values, ROWS - 2 * count, axis=values.ndim - 2)


def swap_halves(values):
    axis = values.ndim - 2
    return jnp.where(
        iota(values.shape, -2) % 2 == 0,
        pltpu.roll(values, ROWS - 1, axis=axis),
        pltpu.roll(values, 1, axis=axis),
    )


def roll_y(values, amount):
    lane = iota(values.shape, -1)
    axis = values.ndim - 1
    if amount == 1:
        moved = pltpu.roll(values, LANES - NZ, axis=axis)
        return jnp.where(lane < LANES - NZ, moved, swap_halves(moved))
    moved = pltpu.roll(values, NZ, axis=axis)
    return jnp.where(lane >= NZ, moved, swap_halves(moved))


def roll_z(values, amount):
    position = iota(values.shape, -1) % NZ
    axis = values.ndim - 1
    if amount == 1:
        return jnp.where(
            position == NZ - 1,
            pltpu.roll(values, NZ - 1, axis=axis),
            pltpu.roll(values, LANES - 1, axis=axis),
        )
    return jnp.where(
        position == 0,
        pltpu.roll(values, LANES - NZ + 1, axis=axis),
        pltpu.roll(values, 1, axis=axis),
    )


def by_pair(choices):
    row = iota(choices[0].shape, -2)
    return jnp.where(
        row < 4,
        jnp.where(row < 2, choices[0], choices[1]),
        jnp.where(row < 6, choices[2], choices[3]),
    )


def product(left, right, left_h=False, right_h=False):
    real = imag = None
    for c in range(3):
        lr, li = (left[0, c], left[1, c]) if left_h else (left[0, :, c], left[1, :, c])
        rr, ri = (right[0, :, c], right[1, :, c]) if right_h else (right[0, c], right[1, c])
        lr, li, rr, ri = lr[:, None], li[:, None], rr[None], ri[None]
        both = lr * rr
        cross = li * ri
        first = lr * ri
        second = li * rr
        re = both + cross if left_h != right_h else both - cross
        if left_h and right_h:
            im = -first - second
        elif left_h:
            im = first - second
        elif right_h:
            im = second - first
        else:
            im = first + second
        real = re if real is None else real + re
        imag = im if imag is None else imag + im
    return jnp.stack([real, imag])


def traceless_part(m):
    parts = [0.5 * (m[0, i, j] - m[0, j, i]) for i, j in UPPER]
    parts += [0.5 * (m[1, i, j] + m[1, j, i]) for i, j in UPPER]
    trace = (m[1, 0, 0] + m[1, 1, 1] + m[1, 2, 2]) * (1.0 / 3.0)
    parts += [m[1, i, i] - trace for i in range(3)]
    return jnp.stack(parts)


def gauge_force(own, plus_t, plus_x, minus_t, minus_x, corner):
    ahead = [plus_t, plus_x, roll_y(own, 1), roll_z(own, 1)]
    behind = [minus_t, minus_x, roll_y(own, -1), roll_z(own, -1)]

    def slanted(arrays, k):
        return by_pair([arrays[(nu - k) % 4] for nu in range(4)])

    diagonal = slanted(behind, 0)
    turned = [
        by_pair([corner, corner, roll_y(plus_t, -1), roll_z(plus_t, -1)]),
        by_pair([corner, corner, roll_y(plus_x, -1), roll_z(plus_x, -1)]),
        roll_y(diagonal, 1),
        roll_z(diagonal, 1),
    ]
    staple = None
    for k in (1, 2, 3):
        up = product(
            product(row_roll(slanted(ahead, k), k), slanted(ahead, 4 - k), right_h=True),
            row_roll(own, k),
            right_h=True,
        )
        low = product(
            product(row_roll(slanted(turned, k), k), slanted(behind, 4 - k), True, True),
            row_roll(diagonal, k),
        )
        staple = up + low if staple is None else staple + up + low
    return (coupling / 3.0) * traceless_part(product(own, staple))


def third_row(two):
    re, im = [], []
    for colour in range(3):
        b, c = (colour + 1) % 3, (colour + 2) % 3
        ar, ai, dr, di = two[0, 0, b], two[1, 0, b], two[0, 1, c], two[1, 1, c]
        er, ei, fr, fi = two[0, 0, c], two[1, 0, c], two[0, 1, b], two[1, 1, b]
        re.append(ar * dr - ai * di - (er * fr - ei * fi))
        im.append(-(ar * di + ai * dr - (er * fi + ei * fr)))
    return jnp.stack([jnp.stack(re), jnp.stack(im)])


def evolve(moment, own):
    a = time_step * moment
    x01, x02, x12 = a[3], a[4], a[5]
    y01, y02, y12 = -a[0], -a[1], -a[2]
    h0, h1, h2 = a[6], a[7], a[8]
    n01 = x01 * x01 + y01 * y01
    n02 = x02 * x02 + y02 * y02
    n12 = x12 * x12 + y12 * y12
    g0 = h0 * h0 + n01 + n02
    g1 = h1 * h1 + n01 + n12
    g2 = h2 * h2 + n02 + n12
    u01 = (h0 + h1) * x01 + (x02 * x12 + y02 * y12)
    v01 = (h0 + h1) * y01 + (y02 * x12 - x02 * y12)
    p02 = x01 * x12 - y01 * y12
    q02 = x01 * y12 + y01 * x12
    u02 = (h0 + h2) * x02 + p02
    v02 = (h0 + h2) * y02 + q02
    u12 = (h1 + h2) * x12 + (x01 * x02 + y01 * y02)
    v12 = (h1 + h2) * y12 + (x01 * y02 - y01 * x02)
    s = 0.5 * (g0 + g1 + g2)
    d = (
        h0 * h1 * h2
        + 2.0 * (p02 * x02 + q02 * y02)
        - h0 * n12
        - h1 * n02
        - h2 * n01
    )
    c0r = 1.0 - d * d * (1.0 / 720.0)
    c0i = d * (s * (1.0 / 120.0) - 1.0 / 6.0)
    c1r = d * (1.0 / 24.0 - s * (1.0 / 360.0))
    c1i = 1.0 + s * (s * (1.0 / 120.0) - 1.0 / 6.0)
    c2r = s * (1.0 / 24.0 - s * (1.0 / 720.0)) - 0.5
    c2i = d * (1.0 / 120.0)
    re = [[None] * 3 for _ in range(3)]
    im = [[None] * 3 for _ in range(3)]
    for i, (h, g) in enumerate(((h0, g0), (h1, g1), (h2, g2))):
        re[i][i] = c0r + c1r * h + c2r * g
        im[i][i] = c0i + c1i * h + c2i * g
    for (i, j), x, y, u, v in (
        ((0, 1), x01, y01, u01, v01),
        ((0, 2), x02, y02, u02, v02),
        ((1, 2), x12, y12, u12, v12),
    ):
        rx = c1r * x + c2r * u
        iy = c1i * y + c2i * v
        ix = c1i * x + c2i * u
        ry = c1r * y + c2r * v
        re[i][j], re[j][i] = rx - iy, rx + iy
        im[i][j], im[j][i] = ix + ry, ix - ry
    e = jnp.stack([jnp.stack([jnp.stack(r) for r in re]), jnp.stack([jnp.stack(r) for r in im])])
    return product(e, own)


def spread(values, pair):
    return by_pair([row_roll(values, pair - p) for p in range(4)])


def matvec(matrix, v, herm=False):
    real = imag = None
    for c in range(3):
        mr, mi = (matrix[0, c], matrix[1, c]) if herm else (matrix[0, :, c], matrix[1, :, c])
        vr, vi = v[0, c][None], v[1, c][None]
        if herm:
            re = mr * vr + mi * vi
            im = mr * vi - mi * vr
        else:
            re = mr * vr - mi * vi
            im = mr * vi + mi * vr
        real = re if real is None else real + re
        imag = im if imag is None else imag + im
    return jnp.stack([real, imag])


def site_links(own):
    return [
        spread(own, 1),
        spread(own, 2),
        spread(roll_y(own, -1), 2),
        spread(own, 3),
        spread(roll_z(own, -1), 3),
    ]


def gather_rows(ref, starts):
    return jnp.concatenate([ref[pl.ds(s, 2), :] for s in starts], axis=0)


def scatter_rows(ref, starts, values):
    for n, s in enumerate(starts):
        ref[pl.ds(s, 2), :] = values[2 * n : 2 * n + 2]


def link_rows(i, j, c):
    return [(((mu * 3 + i) * 3 + j) * 2 + c) * 2 for mu in range(4)]


def vector_rows(tile, a, c, h):
    return [((((4 * tile + n) * 3 + a) * 2 + c) * 2 + h) * 2 for n in range(4)]


def kernel(
    sizes,
    tiles,
    coef,
    links_ref,
    momenta_ref,
    vectors_ref,
    links_out,
    momenta_out,
    vectors_out,
    links_in,
    momenta_in,
    vectors_in,
    two_rows,
    v_in,
    v_done,
    state,
    pair_u,
    got_u,
    got_pair_u,
    send_p,
    pair_p,
    got_p,
    got_pair_p,
    hop_links,
    fields,
    got_fields,
    total,
    partial,
    load_sem,
    send_sem,
    recv_sem,
):
    n_grp, n_ta, n_x = sizes
    ring = n_grp * tiles == n_x and n_x == 4
    grp, ta, x = lax.axis_index("grp"), lax.axis_index("ta"), lax.axis_index("xyz")
    n_t = n_grp * n_ta
    t = grp * n_ta + ta

    def device(dt, dx):
        tt = lax.rem(t + dt + n_t, n_t)
        return (tt // n_ta, lax.rem(tt, n_ta), lax.rem(x + dx + n_x, n_x))

    def beside(dg, dx):
        return (lax.rem(grp + dg, n_grp), ta, lax.rem(x + dx, n_x))

    whole_to = [device(-1, 0), device(0, -1), device(1, 0), device(0, 1)]
    pair_to = [device(1, -1), device(-1, 1)]
    if ring:
        whole_to.append(device(0, 2))
        peers = [device(-1, 0), device(1, 0)] + pair_to
        peers += [beside(dg, dx) for dg in range(n_grp) for dx in range(n_x) if dg or dx]
    else:
        peers = whole_to + pair_to + [beside(1, 0)]
    barrier = pltpu.get_barrier_semaphore()
    for peer in peers:
        pl.semaphore_signal(
            barrier, inc=1, device_id=peer, device_id_type=pl.DeviceIdType.MESH
        )
    loads = [
        pltpu.make_async_copy(links_ref, links_in, load_sem.at[0]),
        pltpu.make_async_copy(vectors_ref, vectors_in, load_sem.at[1]),
        pltpu.make_async_copy(momenta_ref, momenta_in, load_sem.at[2]),
    ]
    for load in loads:
        load.start()

    counter = [0]

    def describe(src, dst, to, send, recv):
        return pltpu.make_async_remote_copy(
            src_ref=src,
            dst_ref=dst,
            send_sem=send_sem.at[send],
            recv_sem=recv_sem.at[recv],
            device_id=to,
            device_id_type=pl.DeviceIdType.MESH,
        )

    def take(count):
        counter[0] += count
        return counter[0] - count

    def copy(src, dst, to):
        n = take(1)
        made = describe(src, dst, to, n, n)
        made.start()
        return made

    pending = []

    loads[0].wait()
    for i in range(3):
        for j in range(3):
            for c in range(2):
                state[0, c, i, j] = gather_rows(links_in, link_rows(i, j, c))
    two_rows[...] = state[0, :, 0:2]
    pair_u[0] = two_rows[:, :, :, 0:2, :]
    pair_u[1] = two_rows[:, :, :, 2:4, :]
    pl.semaphore_wait(barrier, len(peers))

    first = [copy(two_rows, got_u.at[i], whole_to[i]) for i in (1, 3, 0, 2)]
    first += [copy(pair_u.at[i], got_pair_u.at[i], pair_to[i]) for i in range(2)]
    pending += first

    loads[1].wait()
    for h in range(2):
        for tile in range(tiles):
            for c in range(2):
                for a in range(3):
                    v_in[h, tile, c, a] = gather_rows(vectors_in, vector_rows(tile, a, c, h))
    loads[2].wait()
    moment = jnp.stack(
        [gather_rows(momenta_in, link_rows(i, j, 0)) for i, j in UPPER]
        + [gather_rows(momenta_in, link_rows(i, j, 1)) for i, j in UPPER]
        + [gather_rows(momenta_in, link_rows(i, i, 1)) for i in range(3)]
    )
    send_p[0] = moment
    for made in first:
        made.wait_recv()

    if ring:
        far = copy(two_rows, got_u.at[4], whole_to[4])
        pending.append(far)
        own_tile = x // tiles
        home = lax.rem(x, tiles)
        out_send, out_recv = take(2 * tiles), take(n_x)
        moves = []
        for h in range(2):
            for tile in range(tiles):
                target = grp * tiles + tile
                slot = lax.rem(x - target + n_x, n_x)
                here = jnp.logical_and(grp == h, x == target)
                made = describe(
                    v_in.at[h, tile],
                    fields.at[0, slot],
                    (h, ta, target),
                    out_send + h * tiles + tile,
                    out_recv + slot,
                )
                moves.append((here, made))
                pl.when(jnp.logical_not(here))(made.start)

        @pl.when(own_tile == grp)
        def _():
            fields[0, 0] = v_in[grp, home]

    else:
        give = copy(v_in.at[1 - grp], fields.at[0, tiles : 2 * tiles], beside(1, 0))
        fields[0, 0:tiles] = v_in[grp]
        pending.append(give)

    for i in range(4):
        state[i + 1, :, 0:2] = got_u[i]
        state[i + 1, :, 2] = third_row(got_u[i])
    low, high = got_pair_u[0], got_pair_u[1]
    both = jnp.concatenate([low, high, high, high], axis=3)
    state[5, :, 0:2] = both
    state[5, :, 2] = third_row(both)

    def force():
        return gauge_force(*[state[i] for i in range(6)])

    def send_moment(r, moment):
        send_p[r] = moment
        pair_p[r, 0] = moment[:, 0:2, :]
        pair_p[r, 1] = moment[:, 2:4, :]
        made = [copy(send_p.at[r], got_p.at[r, i], whole_to[i]) for i in (1, 3, 0, 2)]
        made += [copy(pair_p.at[r, i], got_pair_p.at[r, i], pair_to[i]) for i in range(2)]
        if ring:
            made.append(copy(send_p.at[r], got_p.at[r, 4], whole_to[4]))
        return made

    def send_fields(r):
        return [
            copy(fields.at[r], got_fields.at[r, 0], whole_to[1]),
            copy(fields.at[r], got_fields.at[r, 1], whole_to[3]),
        ]

    halo = None
    last = []
    moment = send_p[0] - (0.5 * time_step) * force()
    for r in range(NSTEP):
        made = send_moment(r, moment)
        pending += made
        if ring:
            last.append(made.pop())
        elif r == 0:
            give.wait_recv()
            halo = send_fields(0)
            pending += halo
        state[0] = evolve(moment, state[0])
        if ring and r == 1:
            far.wait_recv()
            state[6, :, 0:2] = got_u[4]
            state[6, :, 2] = third_row(got_u[4])
            last[0].wait_recv()
            state[6] = evolve(got_p[0, 4], state[6])
        for one in made:
            one.wait_recv()

        @pl.loop(0, 4)
        def _(i):
            state[i + 1] = evolve(got_p[r, i], state[i + 1])

        low, high = got_pair_p[r, 0], got_pair_p[r, 1]
        state[5] = evolve(jnp.concatenate([low, high, high, high], axis=1), state[5])
        if r + 1 < NSTEP:
            moment = moment - time_step * force()

    def finish_momenta():
        done = moment - (0.5 * time_step) * force()
        zero = jnp.zeros_like(done[0])
        for n, (i, j) in enumerate(UPPER):
            scatter_rows(momenta_out, link_rows(i, j, 0), done[n])
            scatter_rows(momenta_out, link_rows(j, i, 0), -done[n])
            scatter_rows(momenta_out, link_rows(i, j, 1), done[n + 3])
            scatter_rows(momenta_out, link_rows(j, i, 1), done[n + 3])
        for i in range(3):
            scatter_rows(momenta_out, link_rows(i, i, 0), zero)
            scatter_rows(momenta_out, link_rows(i, i, 1), done[6 + i])

    def finish_links():
        for i in range(3):
            for j in range(3):
                for c in range(2):
                    scatter_rows(links_out, link_rows(i, j, c), state[0, c, i, j])

    def step(k, g, acc):
        acc = acc * (-1.0 / 6.0)
        if k == 0:
            fields[1, g] = acc
            total[g] = coef[0] * fields[0, g] + coef[1] * acc
        else:
            following = 2.0 * acc - fields[k - 1, g]
            if k + 1 < NCHEB:
                fields[k + 1, g] = following
            total[g] = total[g] + coef[k + 1] * following

    def hop_local(k, g, at):
        v = fields[k, g]
        acc = matvec(hop_links[at, 1], roll_y(v, 1))
        acc = acc + matvec(hop_links[at, 2], roll_y(v, -1), True)
        acc = acc + matvec(hop_links[at, 3], roll_z(v, 1))
        return acc + matvec(hop_links[at, 4], roll_z(v, -1), True)

    def store_links(at, slot):
        for n, matrix in enumerate(site_links(state[slot])):
            hop_links[at, n] = matrix

    if ring:
        for at, slot in ((0, 0), (1, 2), (3, 4)):
            store_links(at, slot)
        last[1].wait_recv()
        state[6] = evolve(got_p[1, 4], state[6])
        store_links(2, 6)
        for slot in range(n_x):
            waiter = describe(v_in.at[0, 0], fields.at[0, slot], beside(1, 0), 0, out_recv + slot)
            if slot:
                waiter.wait_recv()
            else:
                pl.when(own_tile != grp)(waiter.wait_recv)

        def hop(k, g):
            after, before = (g + 1) % n_x, (g + n_x - 1) % n_x
            acc = hop_local(k, g, g)
            acc = acc + matvec(hop_links[g, 0], fields[k, after])
            acc = acc + matvec(hop_links[before, 0], fields[k, before], True)
            step(k, g, acc)

        for k in range(NCHEB - 1):

            @pl.loop(0, n_x)
            def _(g):
                after, before = lax.rem(g + 1, n_x), lax.rem(g + n_x - 1, n_x)
                acc = hop_local(k, g, g)
                acc = acc + matvec(hop_links[g, 0], fields[k, after])
                acc = acc + matvec(hop_links[before, 0], fields[k, before], True)
                step(k, g, acc)

        back_send, back_recv = take(n_x), take(2 * tiles)
        backs = []
        for g in (2, 1, 3, 0):
            hop(NCHEB - 1, g)
            made = describe(
                total.at[g],
                v_done.at[grp, home],
                (own_tile, ta, lax.rem(x + g, n_x)),
                back_send + g,
                back_recv + grp * tiles + home,
            )
            backs.append((g, made))
            if g:
                made.start()
            else:
                pl.when(own_tile != grp)(made.start)

        @pl.when(own_tile == grp)
        def _():
            v_done[grp, home] = total[0]

        finish_momenta()
        finish_links()
        for h in range(2):
            for tile in range(tiles):
                here, _ = moves[h * tiles + tile]
                waiter = describe(
                    total.at[0],
                    v_done.at[h, tile],
                    beside(1, 0),
                    0,
                    back_recv + h * tiles + tile,
                )
                pl.when(jnp.logical_not(here))(waiter.wait_recv)
        for here, made in moves:
            pl.when(jnp.logical_not(here))(made.wait_send)
        for g, made in backs:
            if g:
                made.wait_send()
            else:
                pl.when(own_tile != grp)(made.wait_send)
    else:
        store_links(0, 0)
        hop_links[1, 0] = spread(state[4], 1)
        finish_links()
        for k in range(NCHEB):
            if k:
                halo = send_fields(k)
                pending += halo
            if k == 1:
                finish_momenta()

            @pl.loop(0, 2 * tiles)
            def _(g):
                partial[g] = hop_local(k, g, 0)

            for one in halo:
                one.wait_recv()

            @pl.loop(0, 2 * tiles)
            def _(g):
                acc = partial[g] + matvec(hop_links[0, 0], got_fields[k, 0, g])
                acc = acc + matvec(hop_links[1, 0], got_fields[k, 1, g], True)
                step(k, g, acc)

        back = copy(total.at[tiles : 2 * tiles], v_done.at[grp], beside(1, 0))
        v_done[grp] = total[0:tiles]
        back.wait_recv()
        pending.append(back)

    for h in range(2):
        for tile in range(tiles):
            for c in range(2):
                for a in range(3):
                    scatter_rows(vectors_out, vector_rows(tile, a, c, h), v_done[h, tile, c, a])
    for one in pending:
        one.wait_send()


def body(sizes, links, momenta, vectors, coefficients):
    tiles = vectors.shape[0] * 2 // ROWS
    groups = 2 * tiles
    copies = 2 * (groups + 4) + 7 + 7 * NSTEP + 2 * NCHEB + 2
    vmem = pl.BlockSpec(memory_space=pltpu.VMEM)
    hbm = pl.BlockSpec(memory_space=pltpu.HBM)
    tile = (ROWS, LANES)
    flat_links = (links.size // LANES, LANES)
    flat_vectors = (vectors.size // LANES, LANES)
    new_links, new_momenta, filtered = pl.pallas_call(
        functools.partial(kernel, sizes, tiles),
        out_shape=(
            jax.ShapeDtypeStruct(flat_links, F32),
            jax.ShapeDtypeStruct(flat_links, F32),
            jax.ShapeDtypeStruct(flat_vectors, F32),
        ),
        in_specs=[pl.BlockSpec(memory_space=pltpu.SMEM)] + [hbm] * 3,
        out_specs=(vmem,) * 3,
        scratch_shapes=[
            pltpu.VMEM(flat_links, F32),
            pltpu.VMEM(flat_links, F32),
            pltpu.VMEM(flat_vectors, F32),
            pltpu.VMEM((2, 2, 3) + tile, F32),
            pltpu.VMEM((2, tiles, 2, 3) + tile, F32),
            pltpu.VMEM((2, tiles, 2, 3) + tile, F32),
            pltpu.VMEM((7, 2, 3, 3) + tile, F32),
            pltpu.VMEM((2, 2, 2, 3, 2, LANES), F32),
            pltpu.VMEM((5, 2, 2, 3) + tile, F32),
            pltpu.VMEM((2, 2, 2, 3, 2, LANES), F32),
            pltpu.VMEM((NSTEP, 9) + tile, F32),
            pltpu.VMEM((NSTEP, 2, 9, 2, LANES), F32),
            pltpu.VMEM((NSTEP, 5, 9) + tile, F32),
            pltpu.VMEM((NSTEP, 2, 9, 2, LANES), F32),
            pltpu.VMEM((4, 5, 2, 3, 3) + tile, F32),
            pltpu.VMEM((NCHEB, groups, 2, 3) + tile, F32),
            pltpu.VMEM((NCHEB, 2, groups, 2, 3) + tile, F32),
            pltpu.VMEM((groups, 2, 3) + tile, F32),
            pltpu.VMEM((groups, 2, 3) + tile, F32),
            pltpu.SemaphoreType.DMA((3,)),
            pltpu.SemaphoreType.DMA((copies,)),
            pltpu.SemaphoreType.DMA((copies,)),
        ],
        compiler_params=pltpu.CompilerParams(
            collective_id=0, has_side_effects=True, vmem_limit_bytes=60 * 1024 * 1024
        ),
    )(
        coefficients,
        links.reshape(flat_links),
        momenta.reshape(flat_links),
        vectors.reshape(flat_vectors),
    )
    return (
        new_links.reshape(links.shape),
        new_momenta.reshape(momenta.shape),
        filtered.reshape(vectors.shape),
    )


def solution(mesh):
    sizes = (mesh.shape["grp"], mesh.shape["ta"], mesh.shape["xyz"])
    link_spec = P(None, None, None, None, ("grp", "ta"), "xyz", None)
    vector_spec = P("grp", None, None, None, "ta", "xyz", None)
    return jax.shard_map(
        functools.partial(body, sizes),
        mesh=mesh,
        in_specs=(link_spec, link_spec, vector_spec, P()),
        out_specs=(link_spec, link_spec, vector_spec),
        check_vma=False,
    )
```

```python
import functools

import jax
import jax.numpy as jnp
from jax import lax
from jax.experimental import pallas as pl
from jax.experimental.pallas import tpu as pltpu
from jax.sharding import PartitionSpec as P

NZ = 32
NSTEP = 2
NCHEB = 3

coupling = 5.7
time_step = 0.1

LANES = 128
ROWS = 8
F32 = jnp.float32
UPPER = ((0, 1), (0, 2), (1, 2))


def iota(shape, dim):
    return lax.broadcasted_iota(jnp.int32, shape, len(shape) + dim)


def row_roll(values, count):
    count = count % 4
    if count == 0:
        return values
    return pltpu.roll(values, ROWS - 2 * count, axis=values.ndim - 2)


def swap_halves(values):
    axis = values.ndim - 2
    return jnp.where(
        iota(values.shape, -2) % 2 == 0,
        pltpu.roll(values, ROWS - 1, axis=axis),
        pltpu.roll(values, 1, axis=axis),
    )


def roll_y(values, amount):
    lane = iota(values.shape, -1)
    axis = values.ndim - 1
    if amount == 1:
        moved = pltpu.roll(values, LANES - NZ, axis=axis)
        return jnp.where(lane < LANES - NZ, moved, swap_halves(moved))
    moved = pltpu.roll(values, NZ, axis=axis)
    return jnp.where(lane >= NZ, moved, swap_halves(moved))


def roll_z(values, amount):
    position = iota(values.shape, -1) % NZ
    axis = values.ndim - 1
    if amount == 1:
        return jnp.where(
            position == NZ - 1,
            pltpu.roll(values, NZ - 1, axis=axis),
            pltpu.roll(values, LANES - 1, axis=axis),
        )
    return jnp.where(
        position == 0,
        pltpu.roll(values, LANES - NZ + 1, axis=axis),
        pltpu.roll(values, 1, axis=axis),
    )


def by_pair(choices):
    row = iota(choices[0].shape, -2)
    return jnp.where(
        row < 4,
        jnp.where(row < 2, choices[0], choices[1]),
        jnp.where(row < 6, choices[2], choices[3]),
    )


def product(left, right, left_h=False, right_h=False):
    real = imag = None
    for c in range(3):
        lr, li = (left[0, c], left[1, c]) if left_h else (left[0, :, c], left[1, :, c])
        rr, ri = (right[0, :, c], right[1, :, c]) if right_h else (right[0, c], right[1, c])
        lr, li, rr, ri = lr[:, None], li[:, None], rr[None], ri[None]
        both = lr * rr
        cross = li * ri
        first = lr * ri
        second = li * rr
        re = both + cross if left_h != right_h else both - cross
        if left_h and right_h:
            im = -first - second
        elif left_h:
            im = first - second
        elif right_h:
            im = second - first
        else:
            im = first + second
        real = re if real is None else real + re
        imag = im if imag is None else imag + im
    return jnp.stack([real, imag])


def traceless_part(m):
    parts = [0.5 * (m[0, i, j] - m[0, j, i]) for i, j in UPPER]
    parts += [0.5 * (m[1, i, j] + m[1, j, i]) for i, j in UPPER]
    trace = (m[1, 0, 0] + m[1, 1, 1] + m[1, 2, 2]) * (1.0 / 3.0)
    parts += [m[1, i, i] - trace for i in range(3)]
    return jnp.stack(parts)


def gauge_force(own, plus_t, plus_x, minus_t, minus_x, corner):
    ahead = [plus_t, plus_x, roll_y(own, 1), roll_z(own, 1)]
    behind = [minus_t, minus_x, roll_y(own, -1), roll_z(own, -1)]

    def slanted(arrays, k):
        return by_pair([arrays[(nu - k) % 4] for nu in range(4)])

    diagonal = slanted(behind, 0)
    turned = [
        by_pair([corner, corner, roll_y(plus_t, -1), roll_z(plus_t, -1)]),
        by_pair([corner, corner, roll_y(plus_x, -1), roll_z(plus_x, -1)]),
        roll_y(diagonal, 1),
        roll_z(diagonal, 1),
    ]
    staple = None
    for k in (1, 2, 3):
        up = product(
            product(row_roll(slanted(ahead, k), k), slanted(ahead, 4 - k), right_h=True),
            row_roll(own, k),
            right_h=True,
        )
        low = product(
            product(row_roll(slanted(turned, k), k), slanted(behind, 4 - k), True, True),
            row_roll(diagonal, k),
        )
        staple = up + low if staple is None else staple + up + low
    return (coupling / 3.0) * traceless_part(product(own, staple))


def third_row(two):
    re, im = [], []
    for colour in range(3):
        b, c = (colour + 1) % 3, (colour + 2) % 3
        ar, ai, dr, di = two[0, 0, b], two[1, 0, b], two[0, 1, c], two[1, 1, c]
        er, ei, fr, fi = two[0, 0, c], two[1, 0, c], two[0, 1, b], two[1, 1, b]
        re.append(ar * dr - ai * di - (er * fr - ei * fi))
        im.append(-(ar * di + ai * dr - (er * fi + ei * fr)))
    return jnp.stack([jnp.stack(re), jnp.stack(im)])


def evolve(moment, own):
    a = time_step * moment
    x01, x02, x12 = a[3], a[4], a[5]
    y01, y02, y12 = -a[0], -a[1], -a[2]
    h0, h1, h2 = a[6], a[7], a[8]
    n01 = x01 * x01 + y01 * y01
    n02 = x02 * x02 + y02 * y02
    n12 = x12 * x12 + y12 * y12
    g0 = h0 * h0 + n01 + n02
    g1 = h1 * h1 + n01 + n12
    g2 = h2 * h2 + n02 + n12
    u01 = (h0 + h1) * x01 + (x02 * x12 + y02 * y12)
    v01 = (h0 + h1) * y01 + (y02 * x12 - x02 * y12)
    p02 = x01 * x12 - y01 * y12
    q02 = x01 * y12 + y01 * x12
    u02 = (h0 + h2) * x02 + p02
    v02 = (h0 + h2) * y02 + q02
    u12 = (h1 + h2) * x12 + (x01 * x02 + y01 * y02)
    v12 = (h1 + h2) * y12 + (x01 * y02 - y01 * x02)
    s = 0.5 * (g0 + g1 + g2)
    d = (
        h0 * h1 * h2
        + 2.0 * (p02 * x02 + q02 * y02)
        - h0 * n12
        - h1 * n02
        - h2 * n01
    )
    c0r = 1.0 - d * d * (1.0 / 720.0)
    c0i = d * (s * (1.0 / 120.0) - 1.0 / 6.0)
    c1r = d * (1.0 / 24.0 - s * (1.0 / 360.0))
    c1i = 1.0 + s * (s * (1.0 / 120.0) - 1.0 / 6.0)
    c2r = s * (1.0 / 24.0 - s * (1.0 / 720.0)) - 0.5
    c2i = d * (1.0 / 120.0)
    re = [[None] * 3 for _ in range(3)]
    im = [[None] * 3 for _ in range(3)]
    for i, (h, g) in enumerate(((h0, g0), (h1, g1), (h2, g2))):
        re[i][i] = c0r + c1r * h + c2r * g
        im[i][i] = c0i + c1i * h + c2i * g
    for (i, j), x, y, u, v in (
        ((0, 1), x01, y01, u01, v01),
        ((0, 2), x02, y02, u02, v02),
        ((1, 2), x12, y12, u12, v12),
    ):
        rx = c1r * x + c2r * u
        iy = c1i * y + c2i * v
        ix = c1i * x + c2i * u
        ry = c1r * y + c2r * v
        re[i][j], re[j][i] = rx - iy, rx + iy
        im[i][j], im[j][i] = ix + ry, ix - ry
    e = jnp.stack([jnp.stack([jnp.stack(r) for r in re]), jnp.stack([jnp.stack(r) for r in im])])
    return product(e, own)


def spread(values, pair):
    return by_pair([row_roll(values, pair - p) for p in range(4)])


def matvec(matrix, v, herm=False):
    real = imag = None
    for c in range(3):
        mr, mi = (matrix[0, c], matrix[1, c]) if herm else (matrix[0, :, c], matrix[1, :, c])
        vr, vi = v[0, c][None], v[1, c][None]
        if herm:
            re = mr * vr + mi * vi
            im = mr * vi - mi * vr
        else:
            re = mr * vr - mi * vi
            im = mr * vi + mi * vr
        real = re if real is None else real + re
        imag = im if imag is None else imag + im
    return jnp.stack([real, imag])


def site_links(own):
    return [
        spread(own, 1),
        spread(own, 2),
        spread(roll_y(own, -1), 2),
        spread(own, 3),
        spread(roll_z(own, -1), 3),
    ]


def gather_rows(ref, starts):
    return jnp.concatenate([ref[pl.ds(s, 2), :] for s in starts], axis=0)


def scatter_rows(ref, starts, values):
    for n, s in enumerate(starts):
        ref[pl.ds(s, 2), :] = values[2 * n : 2 * n + 2]


def link_rows(i, j, c):
    return [(((mu * 3 + i) * 3 + j) * 2 + c) * 2 for mu in range(4)]


def vector_rows(tile, a, c, h):
    return [((((4 * tile + n) * 3 + a) * 2 + c) * 2 + h) * 2 for n in range(4)]


def kernel(
    sizes,
    tiles,
    coef,
    links_ref,
    momenta_ref,
    vectors_ref,
    links_out,
    momenta_out,
    vectors_out,
    links_in,
    momenta_in,
    vectors_in,
    two_rows,
    v_in,
    v_done,
    state,
    pair_u,
    got_u,
    got_pair_u,
    send_p,
    pair_p,
    got_p,
    got_pair_p,
    hop_links,
    fields,
    got_fields,
    total,
    partial,
    load_sem,
    send_sem,
    recv_sem,
):
    n_grp, n_ta, n_x = sizes
    ring = n_grp * tiles == n_x and n_x == 4
    grp, ta, x = lax.axis_index("grp"), lax.axis_index("ta"), lax.axis_index("xyz")
    n_t = n_grp * n_ta
    t = grp * n_ta + ta

    def device(dt, dx):
        tt = lax.rem(t + dt + n_t, n_t)
        return (tt // n_ta, lax.rem(tt, n_ta), lax.rem(x + dx + n_x, n_x))

    def beside(dg, dx):
        return (lax.rem(grp + dg, n_grp), ta, lax.rem(x + dx, n_x))

    whole_to = [device(-1, 0), device(0, -1), device(1, 0), device(0, 1)]
    pair_to = [device(1, -1), device(-1, 1)]
    if ring:
        whole_to.append(device(0, 2))
        peers = [device(-1, 0), device(1, 0)] + pair_to
        peers += [beside(dg, dx) for dg in range(n_grp) for dx in range(n_x) if dg or dx]
    else:
        peers = whole_to + pair_to + [beside(1, 0)]
    barrier = pltpu.get_barrier_semaphore()
    for peer in peers:
        pl.semaphore_signal(
            barrier, inc=1, device_id=peer, device_id_type=pl.DeviceIdType.MESH
        )
    loads = [
        pltpu.make_async_copy(links_ref, links_in, load_sem.at[0]),
        pltpu.make_async_copy(vectors_ref, vectors_in, load_sem.at[1]),
        pltpu.make_async_copy(momenta_ref, momenta_in, load_sem.at[2]),
    ]
    for load in loads:
        load.start()

    counter = [0]

    def describe(src, dst, to, send, recv):
        return pltpu.make_async_remote_copy(
            src_ref=src,
            dst_ref=dst,
            send_sem=send_sem.at[send],
            recv_sem=recv_sem.at[recv],
            device_id=to,
            device_id_type=pl.DeviceIdType.MESH,
        )

    def take(count):
        counter[0] += count
        return counter[0] - count

    def copy(src, dst, to):
        n = take(1)
        made = describe(src, dst, to, n, n)
        made.start()
        return made

    pending = []

    loads[0].wait()
    for i in range(3):
        for j in range(3):
            for c in range(2):
                state[0, c, i, j] = gather_rows(links_in, link_rows(i, j, c))
    two_rows[...] = state[0, :, 0:2]
    pair_u[0] = two_rows[:, :, :, 0:2, :]
    pair_u[1] = two_rows[:, :, :, 2:4, :]
    pl.semaphore_wait(barrier, len(peers))

    first = [copy(two_rows, got_u.at[i], whole_to[i]) for i in (1, 3, 0, 2)]
    first += [copy(pair_u.at[i], got_pair_u.at[i], pair_to[i]) for i in range(2)]
    pending += first

    loads[1].wait()
    for h in range(2):
        for tile in range(tiles):
            for c in range(2):
                for a in range(3):
                    v_in[h, tile, c, a] = gather_rows(vectors_in, vector_rows(tile, a, c, h))
    loads[2].wait()
    moment = jnp.stack(
        [gather_rows(momenta_in, link_rows(i, j, 0)) for i, j in UPPER]
        + [gather_rows(momenta_in, link_rows(i, j, 1)) for i, j in UPPER]
        + [gather_rows(momenta_in, link_rows(i, i, 1)) for i in range(3)]
    )
    send_p[0] = moment
    for made in first:
        made.wait_recv()

    if ring:
        far = copy(two_rows, got_u.at[4], whole_to[4])
        pending.append(far)
        own_tile = x // tiles
        home = lax.rem(x, tiles)
        out_send, out_recv = take(2 * tiles), take(n_x)
        moves = []
        for h in range(2):
            for tile in range(tiles):
                target = grp * tiles + tile
                slot = lax.rem(x - target + n_x, n_x)
                here = jnp.logical_and(grp == h, x == target)
                made = describe(
                    v_in.at[h, tile],
                    fields.at[0, slot],
                    (h, ta, target),
                    out_send + h * tiles + tile,
                    out_recv + slot,
                )
                moves.append((here, made))

        @pl.when(own_tile == grp)
        def _():
            fields[0, 0] = v_in[grp, home]

    else:
        give = copy(v_in.at[1 - grp], fields.at[0, tiles : 2 * tiles], beside(1, 0))
        fields[0, 0:tiles] = v_in[grp]
        pending.append(give)

    for i in range(4):
        state[i + 1, :, 0:2] = got_u[i]
        state[i + 1, :, 2] = third_row(got_u[i])
    low, high = got_pair_u[0], got_pair_u[1]
    both = jnp.concatenate([low, high, high, high], axis=3)
    state[5, :, 0:2] = both
    state[5, :, 2] = third_row(both)

    def force():
        return gauge_force(*[state[i] for i in range(6)])

    def send_moment(r, moment):
        send_p[r] = moment
        pair_p[r, 0] = moment[:, 0:2, :]
        pair_p[r, 1] = moment[:, 2:4, :]
        made = [copy(send_p.at[r], got_p.at[r, i], whole_to[i]) for i in (1, 3, 0, 2)]
        made += [copy(pair_p.at[r, i], got_pair_p.at[r, i], pair_to[i]) for i in range(2)]
        if ring:
            made.append(copy(send_p.at[r], got_p.at[r, 4], whole_to[4]))
        return made

    def send_fields(r):
        return [
            copy(fields.at[r], got_fields.at[r, 0], whole_to[1]),
            copy(fields.at[r], got_fields.at[r, 1], whole_to[3]),
        ]

    halo = None
    last = []
    moment = send_p[0] - (0.5 * time_step) * force()
    for r in range(NSTEP):
        made = send_moment(r, moment)
        pending += made
        if ring:
            last.append(made.pop())
        elif r == 0:
            give.wait_recv()
            halo = send_fields(0)
            pending += halo
        state[0] = evolve(moment, state[0])
        if ring and r == 1:
            far.wait_recv()
            state[6, :, 0:2] = got_u[4]
            state[6, :, 2] = third_row(got_u[4])
            last[0].wait_recv()
            state[6] = evolve(got_p[0, 4], state[6])
        for i, one in ((0, made[2]), (2, made[3])):
            one.wait_recv()
            state[i + 1] = evolve(got_p[r, i], state[i + 1])
        for one in made[4:]:
            one.wait_recv()
        low, high = got_pair_p[r, 0], got_pair_p[r, 1]
        state[5] = evolve(jnp.concatenate([low, high, high, high], axis=1), state[5])
        for i, one in ((1, made[0]), (3, made[1])):
            one.wait_recv()
            state[i + 1] = evolve(got_p[r, i], state[i + 1])
        if ring and r == 0:
            for here, one in moves:
                pl.when(jnp.logical_not(here))(one.start)
        if r + 1 < NSTEP:
            moment = moment - time_step * force()

    def finish_momenta():
        done = moment - (0.5 * time_step) * force()
        zero = jnp.zeros_like(done[0])
        for n, (i, j) in enumerate(UPPER):
            scatter_rows(momenta_out, link_rows(i, j, 0), done[n])
            scatter_rows(momenta_out, link_rows(j, i, 0), -done[n])
            scatter_rows(momenta_out, link_rows(i, j, 1), done[n + 3])
            scatter_rows(momenta_out, link_rows(j, i, 1), done[n + 3])
        for i in range(3):
            scatter_rows(momenta_out, link_rows(i, i, 0), zero)
            scatter_rows(momenta_out, link_rows(i, i, 1), done[6 + i])

    def finish_links():
        for i in range(3):
            for j in range(3):
                for c in range(2):
                    scatter_rows(links_out, link_rows(i, j, c), state[0, c, i, j])

    def step(k, g, acc):
        acc = acc * (-1.0 / 6.0)
        if k == 0:
            fields[1, g] = acc
            total[g] = coef[0] * fields[0, g] + coef[1] * acc
        else:
            following = 2.0 * acc - fields[k - 1, g]
            if k + 1 < NCHEB:
                fields[k + 1, g] = following
            total[g] = total[g] + coef[k + 1] * following

    def hop_local(k, g, at):
        v = fields[k, g]
        acc = matvec(hop_links[at, 1], roll_y(v, 1))
        acc = acc + matvec(hop_links[at, 2], roll_y(v, -1), True)
        acc = acc + matvec(hop_links[at, 3], roll_z(v, 1))
        return acc + matvec(hop_links[at, 4], roll_z(v, -1), True)

    def store_links(at, slot):
        for n, matrix in enumerate(site_links(state[slot])):
            hop_links[at, n] = matrix

    if ring:
        for at, slot in ((0, 0), (1, 2), (3, 4)):
            store_links(at, slot)
        for slot in range(n_x):
            waiter = describe(v_in.at[0, 0], fields.at[0, slot], beside(1, 0), 0, out_recv + slot)
            if slot:
                waiter.wait_recv()
            else:
                pl.when(own_tile != grp)(waiter.wait_recv)

        def hop(k, g):
            after, before = lax.rem(g + 1, n_x), lax.rem(g + n_x - 1, n_x)
            acc = hop_local(k, g, g)
            acc = acc + matvec(hop_links[g, 0], fields[k, after])
            acc = acc + matvec(hop_links[before, 0], fields[k, before], True)
            step(k, g, acc)

        pl.loop(0, 2)(functools.partial(hop, 0))
        last[1].wait_recv()
        state[6] = evolve(got_p[1, 4], state[6])
        store_links(2, 6)
        pl.loop(2, n_x)(functools.partial(hop, 0))
        for k in range(1, NCHEB - 1):
            pl.loop(0, n_x)(functools.partial(hop, k))

        back_send, back_recv = take(n_x), take(2 * tiles)
        backs = []
        for g in (2, 1, 3, 0):
            hop(NCHEB - 1, g)
            made = describe(
                total.at[g],
                v_done.at[grp, home],
                (own_tile, ta, lax.rem(x + g, n_x)),
                back_send + g,
                back_recv + grp * tiles + home,
            )
            backs.append((g, made))
            if g:
                made.start()
            else:
                pl.when(own_tile != grp)(made.start)

        @pl.when(own_tile == grp)
        def _():
            v_done[grp, home] = total[0]

        finish_momenta()
        finish_links()
        for h in range(2):
            for tile in range(tiles):
                here, _ = moves[h * tiles + tile]
                waiter = describe(
                    total.at[0],
                    v_done.at[h, tile],
                    beside(1, 0),
                    0,
                    back_recv + h * tiles + tile,
                )
                pl.when(jnp.logical_not(here))(waiter.wait_recv)
        for here, made in moves:
            pl.when(jnp.logical_not(here))(made.wait_send)
        for g, made in backs:
            if g:
                made.wait_send()
            else:
                pl.when(own_tile != grp)(made.wait_send)
    else:
        store_links(0, 0)
        hop_links[1, 0] = spread(state[4], 1)
        finish_links()
        for k in range(NCHEB):
            if k:
                halo = send_fields(k)
                pending += halo
            if k == 1:
                finish_momenta()

            @pl.loop(0, 2 * tiles)
            def _(g):
                partial[g] = hop_local(k, g, 0)

            for one in halo:
                one.wait_recv()

            @pl.loop(0, 2 * tiles)
            def _(g):
                acc = partial[g] + matvec(hop_links[0, 0], got_fields[k, 0, g])
                acc = acc + matvec(hop_links[1, 0], got_fields[k, 1, g], True)
                step(k, g, acc)

        back = copy(total.at[tiles : 2 * tiles], v_done.at[grp], beside(1, 0))
        v_done[grp] = total[0:tiles]
        back.wait_recv()
        pending.append(back)

    for h in range(2):
        for tile in range(tiles):
            for c in range(2):
                for a in range(3):
                    scatter_rows(vectors_out, vector_rows(tile, a, c, h), v_done[h, tile, c, a])
    for one in pending:
        one.wait_send()


def leave(*refs):
    sem = refs[-1]
    copies = [
        pltpu.make_async_copy(refs[n], refs[n + 3], sem.at[n]) for n in range(3)
    ]
    for one in copies:
        one.start()
    for one in copies:
        one.wait()


def body(sizes, links, momenta, vectors, coefficients):
    tiles = vectors.shape[0] * 2 // ROWS
    groups = 2 * tiles
    copies = 2 * (groups + 4) + 7 + 7 * NSTEP + 2 * NCHEB + 2
    vmem = pl.BlockSpec(memory_space=pltpu.VMEM)
    hbm = pl.BlockSpec(memory_space=pltpu.HBM)
    tile = (ROWS, LANES)
    flat_links = (links.size // LANES, LANES)
    flat_vectors = (vectors.size // LANES, LANES)
    new_links, new_momenta, filtered = pl.pallas_call(
        functools.partial(kernel, sizes, tiles),
        out_shape=(
            pltpu.VMEM(flat_links, F32),
            pltpu.VMEM(flat_links, F32),
            pltpu.VMEM(flat_vectors, F32),
        ),
        in_specs=[pl.BlockSpec(memory_space=pltpu.SMEM)] + [hbm] * 3,
        out_specs=(vmem,) * 3,
        scratch_shapes=[
            pltpu.VMEM(flat_links, F32),
            pltpu.VMEM(flat_links, F32),
            pltpu.VMEM(flat_vectors, F32),
            pltpu.VMEM((2, 2, 3) + tile, F32),
            pltpu.VMEM((2, tiles, 2, 3) + tile, F32),
            pltpu.VMEM((2, tiles, 2, 3) + tile, F32),
            pltpu.VMEM((7, 2, 3, 3) + tile, F32),
            pltpu.VMEM((2, 2, 2, 3, 2, LANES), F32),
            pltpu.VMEM((5, 2, 2, 3) + tile, F32),
            pltpu.VMEM((2, 2, 2, 3, 2, LANES), F32),
            pltpu.VMEM((NSTEP, 9) + tile, F32),
            pltpu.VMEM((NSTEP, 2, 9, 2, LANES), F32),
            pltpu.VMEM((NSTEP, 5, 9) + tile, F32),
            pltpu.VMEM((NSTEP, 2, 9, 2, LANES), F32),
            pltpu.VMEM((4, 5, 2, 3, 3) + tile, F32),
            pltpu.VMEM((NCHEB, groups, 2, 3) + tile, F32),
            pltpu.VMEM((NCHEB, 2, groups, 2, 3) + tile, F32),
            pltpu.VMEM((groups, 2, 3) + tile, F32),
            pltpu.VMEM((groups, 2, 3) + tile, F32),
            pltpu.SemaphoreType.DMA((3,)),
            pltpu.SemaphoreType.DMA((copies,)),
            pltpu.SemaphoreType.DMA((copies,)),
        ],
        compiler_params=pltpu.CompilerParams(
            collective_id=0, has_side_effects=True, vmem_limit_bytes=60 * 1024 * 1024
        ),
    )(
        coefficients,
        links.reshape(flat_links),
        momenta.reshape(flat_links),
        vectors.reshape(flat_vectors),
    )
    new_links, new_momenta, filtered = pl.pallas_call(
        leave,
        out_shape=(
            jax.ShapeDtypeStruct(flat_links, F32),
            jax.ShapeDtypeStruct(flat_links, F32),
            jax.ShapeDtypeStruct(flat_vectors, F32),
        ),
        in_specs=[vmem] * 3,
        out_specs=(hbm,) * 3,
        scratch_shapes=[pltpu.SemaphoreType.DMA((3,))],
    )(new_links, new_momenta, filtered)
    return (
        new_links.reshape(links.shape),
        new_momenta.reshape(momenta.shape),
        filtered.reshape(vectors.shape),
    )


def solution(mesh):
    sizes = (mesh.shape["grp"], mesh.shape["ta"], mesh.shape["xyz"])
    link_spec = P(None, None, None, None, ("grp", "ta"), "xyz", None)
    vector_spec = P("grp", None, None, None, "ta", "xyz", None)
    return jax.shard_map(
        functools.partial(body, sizes),
        mesh=mesh,
        in_specs=(link_spec, link_spec, vector_spec, P()),
        out_specs=(link_spec, link_spec, vector_spec),
        check_vma=False,
    )
```

```python
import functools

import jax
import jax.numpy as jnp
from jax import lax
from jax.experimental import pallas as pl
from jax.experimental.pallas import tpu as pltpu
from jax.sharding import PartitionSpec as P

NZ = 32
NSTEP = 2
NCHEB = 3

coupling = 5.7
time_step = 0.1

LANES = 128
ROWS = 8
F32 = jnp.float32
UPPER = ((0, 1), (0, 2), (1, 2))


def rows_of():
    return lax.broadcasted_iota(jnp.int32, (ROWS, LANES), 0)


def lanes_of():
    return lax.broadcasted_iota(jnp.int32, (ROWS, LANES), 1)


def choose(mask, first, second):
    return jnp.where(jnp.broadcast_to(mask, first.shape), first, second)


def row_roll(values, count):
    count = count % 4
    if count == 0:
        return values
    return pltpu.roll(values, ROWS - 2 * count, axis=values.ndim - 2)


def swap_halves(values):
    axis = values.ndim - 2
    return choose(
        (rows_of() & 1) == 0,
        pltpu.roll(values, ROWS - 1, axis=axis),
        pltpu.roll(values, 1, axis=axis),
    )


def roll_y(values, amount):
    axis = values.ndim - 1
    if amount == 1:
        moved = pltpu.roll(values, LANES - NZ, axis=axis)
        return choose(lanes_of() < LANES - NZ, moved, swap_halves(moved))
    moved = pltpu.roll(values, NZ, axis=axis)
    return choose(lanes_of() >= NZ, moved, swap_halves(moved))


def roll_z(values, amount):
    position = lanes_of() & (NZ - 1)
    axis = values.ndim - 1
    if amount == 1:
        return choose(
            position == NZ - 1,
            pltpu.roll(values, NZ - 1, axis=axis),
            pltpu.roll(values, LANES - 1, axis=axis),
        )
    return choose(
        position == 0,
        pltpu.roll(values, LANES - NZ + 1, axis=axis),
        pltpu.roll(values, 1, axis=axis),
    )


def by_pair(choices):
    row = rows_of()
    low = choices[0] if choices[0] is choices[1] else choose(row < 2, choices[0], choices[1])
    return choose(row < 4, low, choose(row < 6, choices[2], choices[3]))


def product(left, right, left_h=False, right_h=False):
    real = imag = None
    for c in range(3):
        lr, li = (left[0, c], left[1, c]) if left_h else (left[0, :, c], left[1, :, c])
        rr, ri = (right[0, :, c], right[1, :, c]) if right_h else (right[0, c], right[1, c])
        lr, li, rr, ri = lr[:, None], li[:, None], rr[None], ri[None]
        both = lr * rr
        cross = li * ri
        first = lr * ri
        second = li * rr
        re = both + cross if left_h != right_h else both - cross
        if left_h and right_h:
            im = -first - second
        elif left_h:
            im = first - second
        elif right_h:
            im = second - first
        else:
            im = first + second
        real = re if real is None else real + re
        imag = im if imag is None else imag + im
    return jnp.stack([real, imag])


def traceless_part(m):
    parts = [0.5 * (m[0, i, j] - m[0, j, i]) for i, j in UPPER]
    parts += [0.5 * (m[1, i, j] + m[1, j, i]) for i, j in UPPER]
    trace = (m[1, 0, 0] + m[1, 1, 1] + m[1, 2, 2]) * (1.0 / 3.0)
    parts += [m[1, i, i] - trace for i in range(3)]
    return jnp.stack(parts)


def gauge_force(own, plus_t, plus_x, minus_t, minus_x, corner):
    ahead = [plus_t, plus_x, roll_y(own, 1), roll_z(own, 1)]
    behind = [minus_t, minus_x, roll_y(own, -1), roll_z(own, -1)]

    def slanted(arrays, k):
        return by_pair([arrays[(nu - k) % 4] for nu in range(4)])

    diagonal = slanted(behind, 0)
    turned = [
        by_pair([corner, corner, roll_y(plus_t, -1), roll_z(plus_t, -1)]),
        by_pair([corner, corner, roll_y(plus_x, -1), roll_z(plus_x, -1)]),
        roll_y(diagonal, 1),
        roll_z(diagonal, 1),
    ]
    staple = None
    for k in (1, 2, 3):
        up = product(
            product(row_roll(slanted(ahead, k), k), slanted(ahead, 4 - k), right_h=True),
            row_roll(own, k),
            right_h=True,
        )
        low = product(
            product(row_roll(slanted(turned, k), k), slanted(behind, 4 - k), True, True),
            row_roll(diagonal, k),
        )
        staple = up + low if staple is None else staple + up + low
    return (coupling / 3.0) * traceless_part(product(own, staple))


def third_row(two):
    re, im = [], []
    for colour in range(3):
        b, c = (colour + 1) % 3, (colour + 2) % 3
        ar, ai, dr, di = two[0, 0, b], two[1, 0, b], two[0, 1, c], two[1, 1, c]
        er, ei, fr, fi = two[0, 0, c], two[1, 0, c], two[0, 1, b], two[1, 1, b]
        re.append(ar * dr - ai * di - (er * fr - ei * fi))
        im.append(-(ar * di + ai * dr - (er * fi + ei * fr)))
    return jnp.stack([jnp.stack(re), jnp.stack(im)])


def evolve(moment, own):
    a = time_step * moment
    x01, x02, x12 = a[3], a[4], a[5]
    y01, y02, y12 = -a[0], -a[1], -a[2]
    h0, h1, h2 = a[6], a[7], a[8]
    n01 = x01 * x01 + y01 * y01
    n02 = x02 * x02 + y02 * y02
    n12 = x12 * x12 + y12 * y12
    g0 = h0 * h0 + n01 + n02
    g1 = h1 * h1 + n01 + n12
    g2 = h2 * h2 + n02 + n12
    u01 = (h0 + h1) * x01 + (x02 * x12 + y02 * y12)
    v01 = (h0 + h1) * y01 + (y02 * x12 - x02 * y12)
    p02 = x01 * x12 - y01 * y12
    q02 = x01 * y12 + y01 * x12
    u02 = (h0 + h2) * x02 + p02
    v02 = (h0 + h2) * y02 + q02
    u12 = (h1 + h2) * x12 + (x01 * x02 + y01 * y02)
    v12 = (h1 + h2) * y12 + (x01 * y02 - y01 * x02)
    s = 0.5 * (g0 + g1 + g2)
    d = (
        h0 * h1 * h2
        + 2.0 * (p02 * x02 + q02 * y02)
        - h0 * n12
        - h1 * n02
        - h2 * n01
    )
    c0r = 1.0 - d * d * (1.0 / 720.0)
    c0i = d * (s * (1.0 / 120.0) - 1.0 / 6.0)
    c1r = d * (1.0 / 24.0 - s * (1.0 / 360.0))
    c1i = 1.0 + s * (s * (1.0 / 120.0) - 1.0 / 6.0)
    c2r = s * (1.0 / 24.0 - s * (1.0 / 720.0)) - 0.5
    c2i = d * (1.0 / 120.0)
    re = [[None] * 3 for _ in range(3)]
    im = [[None] * 3 for _ in range(3)]
    for i, (h, g) in enumerate(((h0, g0), (h1, g1), (h2, g2))):
        re[i][i] = c0r + c1r * h + c2r * g
        im[i][i] = c0i + c1i * h + c2i * g
    for (i, j), x, y, u, v in (
        ((0, 1), x01, y01, u01, v01),
        ((0, 2), x02, y02, u02, v02),
        ((1, 2), x12, y12, u12, v12),
    ):
        rx = c1r * x + c2r * u
        iy = c1i * y + c2i * v
        ix = c1i * x + c2i * u
        ry = c1r * y + c2r * v
        re[i][j], re[j][i] = rx - iy, rx + iy
        im[i][j], im[j][i] = ix + ry, ix - ry
    e = jnp.stack([jnp.stack([jnp.stack(r) for r in re]), jnp.stack([jnp.stack(r) for r in im])])
    return product(e, own)


def spread(values, pair):
    row = rows_of()
    step = -1 if pair % 2 == 0 else 1
    values = choose((row & 2) == 2 * (pair % 2), values, row_roll(values, step))
    return choose((row & 4) == 4 * (pair // 2), values, row_roll(values, 2))


def matvec(matrix, v, herm=False):
    real = imag = None
    for c in range(3):
        mr, mi = (matrix[0, c], matrix[1, c]) if herm else (matrix[0, :, c], matrix[1, :, c])
        vr, vi = v[0, c][None], v[1, c][None]
        if herm:
            re = mr * vr + mi * vi
            im = mr * vi - mi * vr
        else:
            re = mr * vr - mi * vi
            im = mr * vi + mi * vr
        real = re if real is None else real + re
        imag = im if imag is None else imag + im
    return jnp.stack([real, imag])


def site_links(own):
    return [
        spread(own, 1),
        spread(own, 2),
        spread(roll_y(own, -1), 2),
        spread(own, 3),
        spread(roll_z(own, -1), 3),
    ]


def gather_rows(ref, starts):
    return jnp.concatenate([ref[pl.ds(s, 2), :] for s in starts], axis=0)


def scatter_rows(ref, starts, values):
    for n, s in enumerate(starts):
        ref[pl.ds(s, 2), :] = values[2 * n : 2 * n + 2]


def link_rows(i, j, c):
    return [(((mu * 3 + i) * 3 + j) * 2 + c) * 2 for mu in range(4)]


def vector_rows(tile, a, c, h):
    return [((((4 * tile + n) * 3 + a) * 2 + c) * 2 + h) * 2 for n in range(4)]


def kernel(
    sizes,
    tiles,
    coef,
    links_ref,
    momenta_ref,
    vectors_ref,
    links_out,
    momenta_out,
    vectors_out,
    links_in,
    momenta_in,
    vectors_in,
    two_rows,
    v_in,
    v_done,
    state,
    pair_u,
    got_u,
    got_pair_u,
    send_p,
    pair_p,
    got_p,
    got_pair_p,
    hop_links,
    fields,
    got_fields,
    total,
    partial,
    load_sem,
    send_sem,
    recv_sem,
):
    n_grp, n_ta, n_x = sizes
    ring = n_grp * tiles == n_x and n_x == 4
    grp, ta, x = lax.axis_index("grp"), lax.axis_index("ta"), lax.axis_index("xyz")
    n_t = n_grp * n_ta
    t = grp * n_ta + ta

    def device(dt, dx):
        tt = lax.rem(t + dt + n_t, n_t)
        return (tt // n_ta, lax.rem(tt, n_ta), lax.rem(x + dx + n_x, n_x))

    def beside(dg, dx):
        return (lax.rem(grp + dg, n_grp), ta, lax.rem(x + dx, n_x))

    whole_to = [device(-1, 0), device(0, -1), device(1, 0), device(0, 1)]
    pair_to = [device(1, -1), device(-1, 1)]
    if ring:
        whole_to.append(device(0, 2))
        peers = [device(-1, 0), device(1, 0)] + pair_to
        peers += [beside(dg, dx) for dg in range(n_grp) for dx in range(n_x) if dg or dx]
    else:
        peers = whole_to + pair_to + [beside(1, 0)]
    barrier = pltpu.get_barrier_semaphore()
    for peer in peers:
        pl.semaphore_signal(
            barrier, inc=1, device_id=peer, device_id_type=pl.DeviceIdType.MESH
        )
    loads = [
        pltpu.make_async_copy(links_ref, links_in, load_sem.at[0]),
        pltpu.make_async_copy(vectors_ref, vectors_in, load_sem.at[1]),
        pltpu.make_async_copy(momenta_ref, momenta_in, load_sem.at[2]),
    ]
    for load in loads:
        load.start()
    stores = [
        pltpu.make_async_copy(links_in, links_out, load_sem.at[3]),
        pltpu.make_async_copy(momenta_in, momenta_out, load_sem.at[4]),
        pltpu.make_async_copy(vectors_in, vectors_out, load_sem.at[5]),
    ]

    counter = [0]

    def describe(src, dst, to, send, recv):
        return pltpu.make_async_remote_copy(
            src_ref=src,
            dst_ref=dst,
            send_sem=send_sem.at[send],
            recv_sem=recv_sem.at[recv],
            device_id=to,
            device_id_type=pl.DeviceIdType.MESH,
        )

    def take(count):
        counter[0] += count
        return counter[0] - count

    def copy(src, dst, to):
        n = take(1)
        made = describe(src, dst, to, n, n)
        made.start()
        return made

    pending = []

    loads[0].wait()
    for i in range(3):
        for j in range(3):
            for c in range(2):
                state[0, c, i, j] = gather_rows(links_in, link_rows(i, j, c))
    two_rows[...] = state[0, :, 0:2]
    pair_u[0] = two_rows[:, :, :, 0:2, :]
    pair_u[1] = two_rows[:, :, :, 2:4, :]
    pl.semaphore_wait(barrier, len(peers))

    first = [copy(two_rows, got_u.at[i], whole_to[i]) for i in (1, 3, 0, 2)]
    first += [copy(pair_u.at[i], got_pair_u.at[i], pair_to[i]) for i in range(2)]
    pending += first

    loads[1].wait()
    for h in range(2):
        for tile in range(tiles):
            for c in range(2):
                for a in range(3):
                    v_in[h, tile, c, a] = gather_rows(vectors_in, vector_rows(tile, a, c, h))
    loads[2].wait()
    moment = jnp.stack(
        [gather_rows(momenta_in, link_rows(i, j, 0)) for i, j in UPPER]
        + [gather_rows(momenta_in, link_rows(i, j, 1)) for i, j in UPPER]
        + [gather_rows(momenta_in, link_rows(i, i, 1)) for i in range(3)]
    )
    send_p[0] = moment
    for made in first:
        made.wait_recv()

    if ring:
        far = copy(two_rows, got_u.at[4], whole_to[4])
        pending.append(far)
        own_tile = x // tiles
        home = lax.rem(x, tiles)
        out_send, out_recv = take(2 * tiles), take(n_x)
        moves = []
        for h in range(2):
            for tile in range(tiles):
                target = grp * tiles + tile
                slot = lax.rem(x - target + n_x, n_x)
                here = jnp.logical_and(grp == h, x == target)
                made = describe(
                    v_in.at[h, tile],
                    fields.at[0, slot],
                    (h, ta, target),
                    out_send + h * tiles + tile,
                    out_recv + slot,
                )
                moves.append((here, made))

        @pl.when(own_tile == grp)
        def _():
            fields[0, 0] = v_in[grp, home]

    else:
        give = copy(v_in.at[1 - grp], fields.at[0, tiles : 2 * tiles], beside(1, 0))
        fields[0, 0:tiles] = v_in[grp]
        pending.append(give)

    for i in range(4):
        state[i + 1, :, 0:2] = got_u[i]
        state[i + 1, :, 2] = third_row(got_u[i])
    low, high = got_pair_u[0], got_pair_u[1]
    both = jnp.concatenate([low, high, high, high], axis=3)
    state[5, :, 0:2] = both
    state[5, :, 2] = third_row(both)

    def force():
        return gauge_force(*[state[i] for i in range(6)])

    def send_moment(r, moment):
        send_p[r] = moment
        pair_p[r, 0] = moment[:, 0:2, :]
        pair_p[r, 1] = moment[:, 2:4, :]
        made = [copy(send_p.at[r], got_p.at[r, i], whole_to[i]) for i in (1, 3, 0, 2)]
        made += [copy(pair_p.at[r, i], got_pair_p.at[r, i], pair_to[i]) for i in range(2)]
        if ring:
            made.append(copy(send_p.at[r], got_p.at[r, 4], whole_to[4]))
        return made

    def send_fields(r):
        return [
            copy(fields.at[r], got_fields.at[r, 0], whole_to[1]),
            copy(fields.at[r], got_fields.at[r, 1], whole_to[3]),
        ]

    halo = None
    last = []
    moment = send_p[0] - (0.5 * time_step) * force()
    for r in range(NSTEP):
        made = send_moment(r, moment)
        pending += made
        if ring:
            last.append(made.pop())
        elif r == 0:
            give.wait_recv()
            halo = send_fields(0)
            pending += halo
        state[0] = evolve(moment, state[0])
        if ring and r == 1:
            far.wait_recv()
            state[6, :, 0:2] = got_u[4]
            state[6, :, 2] = third_row(got_u[4])
            last[0].wait_recv()
            state[6] = evolve(got_p[0, 4], state[6])
        for i, one in ((0, made[2]), (2, made[3])):
            one.wait_recv()
            state[i + 1] = evolve(got_p[r, i], state[i + 1])
        for one in made[4:]:
            one.wait_recv()
        low, high = got_pair_p[r, 0], got_pair_p[r, 1]
        state[5] = evolve(jnp.concatenate([low, high, high, high], axis=1), state[5])
        for i, one in ((1, made[0]), (3, made[1])):
            one.wait_recv()
            state[i + 1] = evolve(got_p[r, i], state[i + 1])
        if ring and r == 0:
            for here, one in moves:
                pl.when(jnp.logical_not(here))(one.start)
        if r + 1 < NSTEP:
            moment = moment - time_step * force()

    def finish_momenta():
        done = moment - (0.5 * time_step) * force()
        zero = jnp.zeros_like(done[0])
        for n, (i, j) in enumerate(UPPER):
            scatter_rows(momenta_in, link_rows(i, j, 0), done[n])
            scatter_rows(momenta_in, link_rows(j, i, 0), -done[n])
            scatter_rows(momenta_in, link_rows(i, j, 1), done[n + 3])
            scatter_rows(momenta_in, link_rows(j, i, 1), done[n + 3])
        for i in range(3):
            scatter_rows(momenta_in, link_rows(i, i, 0), zero)
            scatter_rows(momenta_in, link_rows(i, i, 1), done[6 + i])
        stores[1].start()

    def finish_links():
        for i in range(3):
            for j in range(3):
                for c in range(2):
                    scatter_rows(links_in, link_rows(i, j, c), state[0, c, i, j])
        stores[0].start()

    def step(k, g, acc):
        acc = acc * (-1.0 / 6.0)
        if k == 0:
            fields[1, g] = acc
            total[g] = coef[0] * fields[0, g] + coef[1] * acc
        else:
            following = 2.0 * acc - fields[k - 1, g]
            if k + 1 < NCHEB:
                fields[k + 1, g] = following
            total[g] = total[g] + coef[k + 1] * following

    def hop_local(k, g, at):
        v = fields[k, g]
        acc = matvec(hop_links[at, 1], roll_y(v, 1))
        acc = acc + matvec(hop_links[at, 2], roll_y(v, -1), True)
        acc = acc + matvec(hop_links[at, 3], roll_z(v, 1))
        return acc + matvec(hop_links[at, 4], roll_z(v, -1), True)

    def store_links(at, slot):
        for n, matrix in enumerate(site_links(state[slot])):
            hop_links[at, n] = matrix

    if ring:
        for at, slot in ((0, 0), (1, 2), (3, 4)):
            store_links(at, slot)
        for slot in range(n_x):
            waiter = describe(v_in.at[0, 0], fields.at[0, slot], beside(1, 0), 0, out_recv + slot)
            if slot:
                waiter.wait_recv()
            else:
                pl.when(own_tile != grp)(waiter.wait_recv)

        def hop(k, g):
            after, before = lax.rem(g + 1, n_x), lax.rem(g + n_x - 1, n_x)
            acc = hop_local(k, g, g)
            acc = acc + matvec(hop_links[g, 0], fields[k, after])
            acc = acc + matvec(hop_links[before, 0], fields[k, before], True)
            step(k, g, acc)

        pl.loop(0, 2)(functools.partial(hop, 0))
        last[1].wait_recv()
        state[6] = evolve(got_p[1, 4], state[6])
        store_links(2, 6)
        pl.loop(2, n_x)(functools.partial(hop, 0))
        for k in range(1, NCHEB - 1):
            pl.loop(0, n_x)(functools.partial(hop, k))

        back_send, back_recv = take(n_x), take(2 * tiles)
        backs = []
        for g in (2, 1, 3, 0):
            hop(NCHEB - 1, g)
            made = describe(
                total.at[g],
                v_done.at[grp, home],
                (own_tile, ta, lax.rem(x + g, n_x)),
                back_send + g,
                back_recv + grp * tiles + home,
            )
            backs.append((g, made))
            if g:
                made.start()
            else:
                pl.when(own_tile != grp)(made.start)

        @pl.when(own_tile == grp)
        def _():
            v_done[grp, home] = total[0]

        finish_links()
        finish_momenta()
        for h in range(2):
            for tile in range(tiles):
                here, _ = moves[h * tiles + tile]
                waiter = describe(
                    total.at[0],
                    v_done.at[h, tile],
                    beside(1, 0),
                    0,
                    back_recv + h * tiles + tile,
                )
                pl.when(jnp.logical_not(here))(waiter.wait_recv)
        for here, made in moves:
            pl.when(jnp.logical_not(here))(made.wait_send)
        for g, made in backs:
            if g:
                made.wait_send()
            else:
                pl.when(own_tile != grp)(made.wait_send)
    else:
        store_links(0, 0)
        hop_links[1, 0] = spread(state[4], 1)
        finish_links()
        for k in range(NCHEB):
            if k:
                halo = send_fields(k)
                pending += halo
            if k == 1:
                finish_momenta()

            @pl.loop(0, 2 * tiles)
            def _(g):
                partial[g] = hop_local(k, g, 0)

            for one in halo:
                one.wait_recv()

            @pl.loop(0, 2 * tiles)
            def _(g):
                acc = partial[g] + matvec(hop_links[0, 0], got_fields[k, 0, g])
                acc = acc + matvec(hop_links[1, 0], got_fields[k, 1, g], True)
                step(k, g, acc)

        back = copy(total.at[tiles : 2 * tiles], v_done.at[grp], beside(1, 0))
        v_done[grp] = total[0:tiles]
        back.wait_recv()
        pending.append(back)

    for h in range(2):
        for tile in range(tiles):
            for c in range(2):
                for a in range(3):
                    scatter_rows(vectors_in, vector_rows(tile, a, c, h), v_done[h, tile, c, a])
    stores[2].start()
    for one in pending:
        one.wait_send()
    for one in stores:
        one.wait()


def leave(*refs):
    sem = refs[-1]
    copies = [
        pltpu.make_async_copy(refs[n], refs[n + 3], sem.at[n]) for n in range(3)
    ]
    for one in copies:
        one.start()
    for one in copies:
        one.wait()


def body(sizes, links, momenta, vectors, coefficients):
    tiles = vectors.shape[0] * 2 // ROWS
    groups = 2 * tiles
    copies = 2 * (groups + 4) + 7 + 7 * NSTEP + 2 * NCHEB + 2
    hbm = pl.BlockSpec(memory_space=pltpu.HBM)
    tile = (ROWS, LANES)
    flat_links = (links.size // LANES, LANES)
    flat_vectors = (vectors.size // LANES, LANES)
    new_links, new_momenta, filtered = pl.pallas_call(
        functools.partial(kernel, sizes, tiles),
        out_shape=(
            jax.ShapeDtypeStruct(flat_links, F32),
            jax.ShapeDtypeStruct(flat_links, F32),
            jax.ShapeDtypeStruct(flat_vectors, F32),
        ),
        in_specs=[pl.BlockSpec(memory_space=pltpu.SMEM)] + [hbm] * 3,
        out_specs=(hbm,) * 3,
        scratch_shapes=[
            pltpu.VMEM(flat_links, F32),
            pltpu.VMEM(flat_links, F32),
            pltpu.VMEM(flat_vectors, F32),
            pltpu.VMEM((2, 2, 3) + tile, F32),
            pltpu.VMEM((2, tiles, 2, 3) + tile, F32),
            pltpu.VMEM((2, tiles, 2, 3) + tile, F32),
            pltpu.VMEM((7, 2, 3, 3) + tile, F32),
            pltpu.VMEM((2, 2, 2, 3, 2, LANES), F32),
            pltpu.VMEM((5, 2, 2, 3) + tile, F32),
            pltpu.VMEM((2, 2, 2, 3, 2, LANES), F32),
            pltpu.VMEM((NSTEP, 9) + tile, F32),
            pltpu.VMEM((NSTEP, 2, 9, 2, LANES), F32),
            pltpu.VMEM((NSTEP, 5, 9) + tile, F32),
            pltpu.VMEM((NSTEP, 2, 9, 2, LANES), F32),
            pltpu.VMEM((4, 5, 2, 3, 3) + tile, F32),
            pltpu.VMEM((NCHEB, groups, 2, 3) + tile, F32),
            pltpu.VMEM((NCHEB, 2, groups, 2, 3) + tile, F32),
            pltpu.VMEM((groups, 2, 3) + tile, F32),
            pltpu.VMEM((groups, 2, 3) + tile, F32),
            pltpu.SemaphoreType.DMA((6,)),
            pltpu.SemaphoreType.DMA((copies,)),
            pltpu.SemaphoreType.DMA((copies,)),
        ],
        compiler_params=pltpu.CompilerParams(
            collective_id=0, has_side_effects=True, vmem_limit_bytes=60 * 1024 * 1024
        ),
    )(
        coefficients,
        links.reshape(flat_links),
        momenta.reshape(flat_links),
        vectors.reshape(flat_vectors),
    )
    new_links, new_momenta, filtered = pl.pallas_call(
        leave,
        out_shape=(
            jax.ShapeDtypeStruct(flat_links, F32),
            jax.ShapeDtypeStruct(flat_links, F32),
            jax.ShapeDtypeStruct(flat_vectors, F32),
        ),
        in_specs=[hbm] * 3,
        out_specs=(hbm,) * 3,
        scratch_shapes=[pltpu.SemaphoreType.DMA((3,))],
        compiler_params=pltpu.CompilerParams(vmem_limit_bytes=60 * 1024 * 1024),
    )(new_links, new_momenta, filtered)
    return (
        new_links.reshape(links.shape),
        new_momenta.reshape(momenta.shape),
        filtered.reshape(vectors.shape),
    )


def solution(mesh):
    sizes = (mesh.shape["grp"], mesh.shape["ta"], mesh.shape["xyz"])
    link_spec = P(None, None, None, None, ("grp", "ta"), "xyz", None)
    vector_spec = P("grp", None, None, None, "ta", "xyz", None)
    return jax.shard_map(
        functools.partial(body, sizes),
        mesh=mesh,
        in_specs=(link_spec, link_spec, vector_spec, P()),
        out_specs=(link_spec, link_spec, vector_spec),
        check_vma=False,
    )
```

```python
import functools

import jax
import jax.numpy as jnp
from jax import lax
from jax.experimental import pallas as pl
from jax.experimental.pallas import tpu as pltpu
from jax.sharding import PartitionSpec as P

NZ = 32
NSTEP = 2
NCHEB = 3

coupling = 5.7
time_step = 0.1

LANES = 128
ROWS = 8
F32 = jnp.float32
UPPER = ((0, 1), (0, 2), (1, 2))


def rows_of():
    return lax.broadcasted_iota(jnp.int32, (ROWS, LANES), 0)


def lanes_of():
    return lax.broadcasted_iota(jnp.int32, (ROWS, LANES), 1)


def choose(mask, first, second):
    return jnp.where(jnp.broadcast_to(mask, first.shape), first, second)


def row_roll(values, count):
    count = count % 4
    if count == 0:
        return values
    return pltpu.roll(values, ROWS - 2 * count, axis=values.ndim - 2)


def swap_halves(values):
    axis = values.ndim - 2
    return choose(
        (rows_of() & 1) == 0,
        pltpu.roll(values, ROWS - 1, axis=axis),
        pltpu.roll(values, 1, axis=axis),
    )


def roll_y(values, amount):
    axis = values.ndim - 1
    if amount == 1:
        moved = pltpu.roll(values, LANES - NZ, axis=axis)
        return choose(lanes_of() < LANES - NZ, moved, swap_halves(moved))
    moved = pltpu.roll(values, NZ, axis=axis)
    return choose(lanes_of() >= NZ, moved, swap_halves(moved))


def roll_z(values, amount):
    position = lanes_of() & (NZ - 1)
    axis = values.ndim - 1
    if amount == 1:
        return choose(
            position == NZ - 1,
            pltpu.roll(values, NZ - 1, axis=axis),
            pltpu.roll(values, LANES - 1, axis=axis),
        )
    return choose(
        position == 0,
        pltpu.roll(values, LANES - NZ + 1, axis=axis),
        pltpu.roll(values, 1, axis=axis),
    )


def by_pair(choices):
    row = rows_of()
    low = choices[0] if choices[0] is choices[1] else choose(row < 2, choices[0], choices[1])
    return choose(row < 4, low, choose(row < 6, choices[2], choices[3]))


def product(left, right, left_h=False, right_h=False):
    real = imag = None
    for c in range(3):
        lr, li = (left[0, c], left[1, c]) if left_h else (left[0, :, c], left[1, :, c])
        rr, ri = (right[0, :, c], right[1, :, c]) if right_h else (right[0, c], right[1, c])
        lr, li, rr, ri = lr[:, None], li[:, None], rr[None], ri[None]
        both = lr * rr
        cross = li * ri
        first = lr * ri
        second = li * rr
        re = both + cross if left_h != right_h else both - cross
        if left_h and right_h:
            im = -first - second
        elif left_h:
            im = first - second
        elif right_h:
            im = second - first
        else:
            im = first + second
        real = re if real is None else real + re
        imag = im if imag is None else imag + im
    return jnp.stack([real, imag])


def traceless_part(m):
    parts = [0.5 * (m[0, i, j] - m[0, j, i]) for i, j in UPPER]
    parts += [0.5 * (m[1, i, j] + m[1, j, i]) for i, j in UPPER]
    trace = (m[1, 0, 0] + m[1, 1, 1] + m[1, 2, 2]) * (1.0 / 3.0)
    parts += [m[1, i, i] - trace for i in range(3)]
    return jnp.stack(parts)


def gauge_force(own, plus_t, plus_x, minus_t, minus_x, corner):
    ahead = [plus_t, plus_x, roll_y(own, 1), roll_z(own, 1)]
    behind = [minus_t, minus_x, roll_y(own, -1), roll_z(own, -1)]

    def slanted(arrays, k):
        return by_pair([arrays[(nu - k) % 4] for nu in range(4)])

    diagonal = slanted(behind, 0)
    turned = [
        by_pair([corner, corner, roll_y(plus_t, -1), roll_z(plus_t, -1)]),
        by_pair([corner, corner, roll_y(plus_x, -1), roll_z(plus_x, -1)]),
        roll_y(diagonal, 1),
        roll_z(diagonal, 1),
    ]
    staple = None
    for k in (1, 2, 3):
        up = product(
            product(row_roll(slanted(ahead, k), k), slanted(ahead, 4 - k), right_h=True),
            row_roll(own, k),
            right_h=True,
        )
        low = product(
            product(row_roll(slanted(turned, k), k), slanted(behind, 4 - k), True, True),
            row_roll(diagonal, k),
        )
        staple = up + low if staple is None else staple + up + low
    return (coupling / 3.0) * traceless_part(product(own, staple))


def third_row(two):
    re, im = [], []
    for colour in range(3):
        b, c = (colour + 1) % 3, (colour + 2) % 3
        ar, ai, dr, di = two[0, 0, b], two[1, 0, b], two[0, 1, c], two[1, 1, c]
        er, ei, fr, fi = two[0, 0, c], two[1, 0, c], two[0, 1, b], two[1, 1, b]
        re.append(ar * dr - ai * di - (er * fr - ei * fi))
        im.append(-(ar * di + ai * dr - (er * fi + ei * fr)))
    return jnp.stack([jnp.stack(re), jnp.stack(im)])


def evolve(moment, own):
    a = time_step * moment
    x01, x02, x12 = a[3], a[4], a[5]
    y01, y02, y12 = -a[0], -a[1], -a[2]
    h0, h1, h2 = a[6], a[7], a[8]
    n01 = x01 * x01 + y01 * y01
    n02 = x02 * x02 + y02 * y02
    n12 = x12 * x12 + y12 * y12
    g0 = h0 * h0 + n01 + n02
    g1 = h1 * h1 + n01 + n12
    g2 = h2 * h2 + n02 + n12
    u01 = (h0 + h1) * x01 + (x02 * x12 + y02 * y12)
    v01 = (h0 + h1) * y01 + (y02 * x12 - x02 * y12)
    p02 = x01 * x12 - y01 * y12
    q02 = x01 * y12 + y01 * x12
    u02 = (h0 + h2) * x02 + p02
    v02 = (h0 + h2) * y02 + q02
    u12 = (h1 + h2) * x12 + (x01 * x02 + y01 * y02)
    v12 = (h1 + h2) * y12 + (x01 * y02 - y01 * x02)
    s = 0.5 * (g0 + g1 + g2)
    d = (
        h0 * h1 * h2
        + 2.0 * (p02 * x02 + q02 * y02)
        - h0 * n12
        - h1 * n02
        - h2 * n01
    )
    c0r = 1.0 - d * d * (1.0 / 720.0)
    c0i = d * (s * (1.0 / 120.0) - 1.0 / 6.0)
    c1r = d * (1.0 / 24.0 - s * (1.0 / 360.0))
    c1i = 1.0 + s * (s * (1.0 / 120.0) - 1.0 / 6.0)
    c2r = s * (1.0 / 24.0 - s * (1.0 / 720.0)) - 0.5
    c2i = d * (1.0 / 120.0)
    re = [[None] * 3 for _ in range(3)]
    im = [[None] * 3 for _ in range(3)]
    for i, (h, g) in enumerate(((h0, g0), (h1, g1), (h2, g2))):
        re[i][i] = c0r + c1r * h + c2r * g
        im[i][i] = c0i + c1i * h + c2i * g
    for (i, j), x, y, u, v in (
        ((0, 1), x01, y01, u01, v01),
        ((0, 2), x02, y02, u02, v02),
        ((1, 2), x12, y12, u12, v12),
    ):
        rx = c1r * x + c2r * u
        iy = c1i * y + c2i * v
        ix = c1i * x + c2i * u
        ry = c1r * y + c2r * v
        re[i][j], re[j][i] = rx - iy, rx + iy
        im[i][j], im[j][i] = ix + ry, ix - ry
    e = jnp.stack([jnp.stack([jnp.stack(r) for r in re]), jnp.stack([jnp.stack(r) for r in im])])
    return product(e, own)


def spread(values, pair):
    row = rows_of()
    step = -1 if pair % 2 == 0 else 1
    values = choose((row & 2) == 2 * (pair % 2), values, row_roll(values, step))
    return choose((row & 4) == 4 * (pair // 2), values, row_roll(values, 2))


def matvec(matrix, v, herm=False):
    real = imag = None
    for c in range(3):
        mr, mi = (matrix[0, c], matrix[1, c]) if herm else (matrix[0, :, c], matrix[1, :, c])
        vr, vi = v[0, c][None], v[1, c][None]
        if herm:
            re = mr * vr + mi * vi
            im = mr * vi - mi * vr
        else:
            re = mr * vr - mi * vi
            im = mr * vi + mi * vr
        real = re if real is None else real + re
        imag = im if imag is None else imag + im
    return jnp.stack([real, imag])


def site_links(own):
    return [
        spread(own, 1),
        spread(own, 2),
        spread(roll_y(own, -1), 2),
        spread(own, 3),
        spread(roll_z(own, -1), 3),
    ]


def gather_rows(ref, starts):
    return jnp.concatenate([ref[pl.ds(s, 2), :] for s in starts], axis=0)


def scatter_rows(ref, starts, values):
    for n, s in enumerate(starts):
        ref[pl.ds(s, 2), :] = values[2 * n : 2 * n + 2]


def link_rows(i, j, c):
    return [(((mu * 3 + i) * 3 + j) * 2 + c) * 2 for mu in range(4)]


def vector_rows(tile, a, c, h):
    return [((((4 * tile + n) * 3 + a) * 2 + c) * 2 + h) * 2 for n in range(4)]


def kernel(
    sizes,
    tiles,
    coef,
    links_ref,
    momenta_ref,
    vectors_ref,
    links_out,
    momenta_out,
    vectors_out,
    links_in,
    momenta_in,
    vectors_in,
    two_rows,
    v_in,
    v_done,
    state,
    pair_u,
    got_u,
    got_pair_u,
    send_p,
    pair_p,
    got_p,
    got_pair_p,
    far_u,
    got_far,
    hop_links,
    fields,
    got_fields,
    total,
    partial,
    load_sem,
    send_sem,
    recv_sem,
):
    n_grp, n_ta, n_x = sizes
    ring = n_grp * tiles == n_x and n_x == 4
    grp, ta, x = lax.axis_index("grp"), lax.axis_index("ta"), lax.axis_index("xyz")
    n_t = n_grp * n_ta
    t = grp * n_ta + ta

    def device(dt, dx):
        tt = lax.rem(t + dt + n_t, n_t)
        return (tt // n_ta, lax.rem(tt, n_ta), lax.rem(x + dx + n_x, n_x))

    def beside(dg, dx):
        return (lax.rem(grp + dg, n_grp), ta, lax.rem(x + dx, n_x))

    whole_to = [device(-1, 0), device(0, -1), device(1, 0), device(0, 1)]
    pair_to = [device(1, -1), device(-1, 1)]
    if ring:
        whole_to.append(device(0, 2))
        peers = [device(-1, 0), device(1, 0)] + pair_to
        peers += [beside(dg, dx) for dg in range(n_grp) for dx in range(n_x) if dg or dx]
    else:
        peers = whole_to + pair_to + [beside(1, 0)]
    barrier = pltpu.get_barrier_semaphore()
    for peer in peers:
        pl.semaphore_signal(
            barrier, inc=1, device_id=peer, device_id_type=pl.DeviceIdType.MESH
        )
    loads = [
        pltpu.make_async_copy(links_ref, links_in, load_sem.at[0]),
        pltpu.make_async_copy(vectors_ref, vectors_in, load_sem.at[1]),
        pltpu.make_async_copy(momenta_ref, momenta_in, load_sem.at[2]),
    ]
    for load in loads:
        load.start()
    stores = [
        pltpu.make_async_copy(links_in, links_out, load_sem.at[3]),
        pltpu.make_async_copy(momenta_in, momenta_out, load_sem.at[4]),
        pltpu.make_async_copy(vectors_in, vectors_out, load_sem.at[5]),
    ]

    counter = [0]

    def describe(src, dst, to, send, recv):
        return pltpu.make_async_remote_copy(
            src_ref=src,
            dst_ref=dst,
            send_sem=send_sem.at[send],
            recv_sem=recv_sem.at[recv],
            device_id=to,
            device_id_type=pl.DeviceIdType.MESH,
        )

    def take(count):
        counter[0] += count
        return counter[0] - count

    def copy(src, dst, to):
        n = take(1)
        made = describe(src, dst, to, n, n)
        made.start()
        return made

    pending = []

    loads[0].wait()
    for i in range(3):
        for j in range(3):
            for c in range(2):
                state[0, c, i, j] = gather_rows(links_in, link_rows(i, j, c))
    two_rows[...] = state[0, :, 0:2]
    pair_u[0] = two_rows[:, :, :, 0:2, :]
    pair_u[1] = two_rows[:, :, :, 2:4, :]
    pl.semaphore_wait(barrier, len(peers))

    first = [copy(two_rows, got_u.at[i], whole_to[i]) for i in (1, 3, 0, 2)]
    first += [copy(pair_u.at[i], got_pair_u.at[i], pair_to[i]) for i in range(2)]
    pending += first

    loads[1].wait()
    for h in range(2):
        for tile in range(tiles):
            for c in range(2):
                for a in range(3):
                    v_in[h, tile, c, a] = gather_rows(vectors_in, vector_rows(tile, a, c, h))
    loads[2].wait()
    moment = jnp.stack(
        [gather_rows(momenta_in, link_rows(i, j, 0)) for i, j in UPPER]
        + [gather_rows(momenta_in, link_rows(i, j, 1)) for i, j in UPPER]
        + [gather_rows(momenta_in, link_rows(i, i, 1)) for i in range(3)]
    )
    send_p[0] = moment
    for made in first:
        made.wait_recv()

    if ring:
        own_tile = x // tiles
        home = lax.rem(x, tiles)
        out_send, out_recv = take(2 * tiles), take(n_x)
        moves = []
        for h in range(2):
            for tile in range(tiles):
                target = grp * tiles + tile
                slot = lax.rem(x - target + n_x, n_x)
                here = jnp.logical_and(grp == h, x == target)
                made = describe(
                    v_in.at[h, tile],
                    fields.at[0, slot],
                    (h, ta, target),
                    out_send + h * tiles + tile,
                    out_recv + slot,
                )
                moves.append((here, made))

        @pl.when(own_tile == grp)
        def _():
            fields[0, 0] = v_in[grp, home]

    else:
        give = copy(v_in.at[1 - grp], fields.at[0, tiles : 2 * tiles], beside(1, 0))
        fields[0, 0:tiles] = v_in[grp]
        pending.append(give)

    for i in range(4):
        state[i + 1, :, 0:2] = got_u[i]
        state[i + 1, :, 2] = third_row(got_u[i])
    low, high = got_pair_u[0], got_pair_u[1]
    both = jnp.concatenate([low, high, high, high], axis=3)
    state[5, :, 0:2] = both
    state[5, :, 2] = third_row(both)

    def force():
        return gauge_force(*[state[i] for i in range(6)])

    def send_moment(r, moment):
        send_p[r] = moment
        pair_p[r, 0] = moment[:, 0:2, :]
        pair_p[r, 1] = moment[:, 2:4, :]
        made = [copy(send_p.at[r], got_p.at[r, i], whole_to[i]) for i in (1, 3, 0, 2)]
        made += [copy(pair_p.at[r, i], got_pair_p.at[r, i], pair_to[i]) for i in range(2)]
        return made

    def send_fields(r):
        return [
            copy(fields.at[r], got_fields.at[r, 0], whole_to[1]),
            copy(fields.at[r], got_fields.at[r, 1], whole_to[3]),
        ]

    halo = None
    entries = [(c, i, j) for c in range(2) for i in range(3) for j in range(3)]

    def far_rows(n):
        return [2 * (len(entries) * d + n) for d in range(3)]

    moment = send_p[0] - (0.5 * time_step) * force()
    for r in range(NSTEP):
        made = send_moment(r, moment)
        pending += made
        if r == 0 and not ring:
            give.wait_recv()
            halo = send_fields(0)
            pending += halo
        state[0] = evolve(moment, state[0])
        if ring and r + 1 == NSTEP:
            for n, (c, i, j) in enumerate(entries):
                scatter_rows(far_u, far_rows(n), state[0, c, i, j][2:])
            far_u[pl.ds(6 * len(entries), 4), :] = jnp.zeros((4, LANES), F32)
            far = copy(far_u, got_far, whole_to[4])
            pending.append(far)
        for i, one in ((0, made[2]), (2, made[3])):
            one.wait_recv()
            state[i + 1] = evolve(got_p[r, i], state[i + 1])
        for one in made[4:]:
            one.wait_recv()
        low, high = got_pair_p[r, 0], got_pair_p[r, 1]
        state[5] = evolve(jnp.concatenate([low, high, high, high], axis=1), state[5])
        for i, one in ((1, made[0]), (3, made[1])):
            one.wait_recv()
            state[i + 1] = evolve(got_p[r, i], state[i + 1])
        if ring and r == 0:
            for here, one in moves:
                pl.when(jnp.logical_not(here))(one.start)
        if r + 1 < NSTEP:
            moment = moment - time_step * force()

    def finish_momenta():
        done = moment - (0.5 * time_step) * force()
        zero = jnp.zeros_like(done[0])
        for n, (i, j) in enumerate(UPPER):
            scatter_rows(momenta_in, link_rows(i, j, 0), done[n])
            scatter_rows(momenta_in, link_rows(j, i, 0), -done[n])
            scatter_rows(momenta_in, link_rows(i, j, 1), done[n + 3])
            scatter_rows(momenta_in, link_rows(j, i, 1), done[n + 3])
        for i in range(3):
            scatter_rows(momenta_in, link_rows(i, i, 0), zero)
            scatter_rows(momenta_in, link_rows(i, i, 1), done[6 + i])
        stores[1].start()

    def finish_links():
        for i in range(3):
            for j in range(3):
                for c in range(2):
                    scatter_rows(links_in, link_rows(i, j, c), state[0, c, i, j])
        stores[0].start()

    def step(k, g, acc):
        acc = acc * (-1.0 / 6.0)
        if k == 0:
            fields[1, g] = acc
            total[g] = coef[0] * fields[0, g] + coef[1] * acc
        else:
            following = 2.0 * acc - fields[k - 1, g]
            if k + 1 < NCHEB:
                fields[k + 1, g] = following
            total[g] = total[g] + coef[k + 1] * following

    def hop_local(k, g, at):
        v = fields[k, g]
        acc = matvec(hop_links[at, 1], roll_y(v, 1))
        acc = acc + matvec(hop_links[at, 2], roll_y(v, -1), True)
        acc = acc + matvec(hop_links[at, 3], roll_z(v, 1))
        return acc + matvec(hop_links[at, 4], roll_z(v, -1), True)

    def store_links(at, slot):
        for n, matrix in enumerate(site_links(state[slot])):
            hop_links[at, n] = matrix

    if ring:
        for at, slot in ((0, 0), (1, 2), (3, 4)):
            store_links(at, slot)
        for slot in range(n_x):
            waiter = describe(v_in.at[0, 0], fields.at[0, slot], beside(1, 0), 0, out_recv + slot)
            if slot:
                waiter.wait_recv()
            else:
                pl.when(own_tile != grp)(waiter.wait_recv)

        def hop(k, g):
            after, before = lax.rem(g + 1, n_x), lax.rem(g + n_x - 1, n_x)
            acc = hop_local(k, g, g)
            acc = acc + matvec(hop_links[g, 0], fields[k, after])
            acc = acc + matvec(hop_links[before, 0], fields[k, before], True)
            step(k, g, acc)

        pl.loop(0, 2)(functools.partial(hop, 0))
        far.wait_recv()
        for n, (c, i, j) in enumerate(entries):
            starts = far_rows(n)
            state[6, c, i, j] = gather_rows(got_far, starts[:1] + starts)
        store_links(2, 6)
        pl.loop(2, n_x)(functools.partial(hop, 0))
        for k in range(1, NCHEB - 1):
            pl.loop(0, n_x)(functools.partial(hop, k))

        back_send, back_recv = take(n_x), take(2 * tiles)
        backs = []
        for g in (2, 1, 3, 0):
            hop(NCHEB - 1, g)
            made = describe(
                total.at[g],
                v_done.at[grp, home],
                (own_tile, ta, lax.rem(x + g, n_x)),
                back_send + g,
                back_recv + grp * tiles + home,
            )
            backs.append((g, made))
            if g:
                made.start()
            else:
                pl.when(own_tile != grp)(made.start)

        @pl.when(own_tile == grp)
        def _():
            v_done[grp, home] = total[0]

        finish_links()
        finish_momenta()
        for h in range(2):
            for tile in range(tiles):
                here, _ = moves[h * tiles + tile]
                waiter = describe(
                    total.at[0],
                    v_done.at[h, tile],
                    beside(1, 0),
                    0,
                    back_recv + h * tiles + tile,
                )
                pl.when(jnp.logical_not(here))(waiter.wait_recv)
        for here, made in moves:
            pl.when(jnp.logical_not(here))(made.wait_send)
        for g, made in backs:
            if g:
                made.wait_send()
            else:
                pl.when(own_tile != grp)(made.wait_send)
    else:
        store_links(0, 0)
        hop_links[1, 0] = spread(state[4], 1)
        finish_links()
        for k in range(NCHEB):
            if k:
                halo = send_fields(k)
                pending += halo
            if k == 1:
                finish_momenta()

            @pl.loop(0, 2 * tiles)
            def _(g):
                partial[g] = hop_local(k, g, 0)

            for one in halo:
                one.wait_recv()

            @pl.loop(0, 2 * tiles)
            def _(g):
                acc = partial[g] + matvec(hop_links[0, 0], got_fields[k, 0, g])
                acc = acc + matvec(hop_links[1, 0], got_fields[k, 1, g], True)
                step(k, g, acc)

        back = copy(total.at[tiles : 2 * tiles], v_done.at[grp], beside(1, 0))
        v_done[grp] = total[0:tiles]
        back.wait_recv()
        pending.append(back)

    for h in range(2):
        for tile in range(tiles):
            for c in range(2):
                for a in range(3):
                    scatter_rows(vectors_in, vector_rows(tile, a, c, h), v_done[h, tile, c, a])
    stores[2].start()
    for one in pending:
        one.wait_send()
    for one in stores:
        one.wait()


def leave(*refs):
    ins, outs, held, sem = refs[0:3], refs[3:6], refs[6:9], refs[9]
    loads = [pltpu.make_async_copy(ins[n], held[n], sem.at[n]) for n in range(3)]
    stores = [pltpu.make_async_copy(held[n], outs[n], sem.at[n + 3]) for n in range(3)]
    for one in loads:
        one.start()
    for load, store in zip(loads, stores):
        load.wait()
        store.start()
    for one in stores:
        one.wait()


def body(sizes, links, momenta, vectors, coefficients):
    tiles = vectors.shape[0] * 2 // ROWS
    groups = 2 * tiles
    copies = 2 * (groups + 4) + 7 + 7 * NSTEP + 2 * NCHEB + 2
    hbm = pl.BlockSpec(memory_space=pltpu.HBM)
    tile = (ROWS, LANES)
    flat_links = (links.size // LANES, LANES)
    flat_vectors = (vectors.size // LANES, LANES)
    new_links, new_momenta, filtered = pl.pallas_call(
        functools.partial(kernel, sizes, tiles),
        out_shape=(
            jax.ShapeDtypeStruct(flat_links, F32),
            jax.ShapeDtypeStruct(flat_links, F32),
            jax.ShapeDtypeStruct(flat_vectors, F32),
        ),
        in_specs=[pl.BlockSpec(memory_space=pltpu.SMEM)] + [hbm] * 3,
        out_specs=(hbm,) * 3,
        scratch_shapes=[
            pltpu.VMEM(flat_links, F32),
            pltpu.VMEM(flat_links, F32),
            pltpu.VMEM(flat_vectors, F32),
            pltpu.VMEM((2, 2, 3) + tile, F32),
            pltpu.VMEM((2, tiles, 2, 3) + tile, F32),
            pltpu.VMEM((2, tiles, 2, 3) + tile, F32),
            pltpu.VMEM((7, 2, 3, 3) + tile, F32),
            pltpu.VMEM((2, 2, 2, 3, 2, LANES), F32),
            pltpu.VMEM((4, 2, 2, 3) + tile, F32),
            pltpu.VMEM((2, 2, 2, 3, 2, LANES), F32),
            pltpu.VMEM((NSTEP, 9) + tile, F32),
            pltpu.VMEM((NSTEP, 2, 9, 2, LANES), F32),
            pltpu.VMEM((NSTEP, 4, 9) + tile, F32),
            pltpu.VMEM((NSTEP, 2, 9, 2, LANES), F32),
            pltpu.VMEM((112, LANES), F32),
            pltpu.VMEM((112, LANES), F32),
            pltpu.VMEM((4, 5, 2, 3, 3) + tile, F32),
            pltpu.VMEM((NCHEB, groups, 2, 3) + tile, F32),
            pltpu.VMEM((NCHEB, 2, groups, 2, 3) + tile, F32),
            pltpu.VMEM((groups, 2, 3) + tile, F32),
            pltpu.VMEM((groups, 2, 3) + tile, F32),
            pltpu.SemaphoreType.DMA((6,)),
            pltpu.SemaphoreType.DMA((copies,)),
            pltpu.SemaphoreType.DMA((copies,)),
        ],
        compiler_params=pltpu.CompilerParams(
            collective_id=0, has_side_effects=True, vmem_limit_bytes=60 * 1024 * 1024
        ),
    )(
        coefficients,
        links.reshape(flat_links),
        momenta.reshape(flat_links),
        vectors.reshape(flat_vectors),
    )
    new_links, new_momenta, filtered = pl.pallas_call(
        leave,
        out_shape=(
            jax.ShapeDtypeStruct(flat_links, F32),
            jax.ShapeDtypeStruct(flat_links, F32),
            jax.ShapeDtypeStruct(flat_vectors, F32),
        ),
        in_specs=[hbm] * 3,
        out_specs=(hbm,) * 3,
        scratch_shapes=[
            pltpu.VMEM(flat_links, F32),
            pltpu.VMEM(flat_links, F32),
            pltpu.VMEM(flat_vectors, F32),
            pltpu.SemaphoreType.DMA((6,)),
        ],
        compiler_params=pltpu.CompilerParams(vmem_limit_bytes=60 * 1024 * 1024),
    )(new_links, new_momenta, filtered)
    return (
        new_links.reshape(links.shape),
        new_momenta.reshape(momenta.shape),
        filtered.reshape(vectors.shape),
    )


def solution(mesh):
    sizes = (mesh.shape["grp"], mesh.shape["ta"], mesh.shape["xyz"])
    link_spec = P(None, None, None, None, ("grp", "ta"), "xyz", None)
    vector_spec = P("grp", None, None, None, "ta", "xyz", None)
    return jax.shard_map(
        functools.partial(body, sizes),
        mesh=mesh,
        in_specs=(link_spec, link_spec, vector_spec, P()),
        out_specs=(link_spec, link_spec, vector_spec),
        check_vma=False,
    )
```

```python
import functools

import jax
import jax.numpy as jnp
from jax import lax
from jax.experimental import pallas as pl
from jax.experimental.pallas import tpu as pltpu
from jax.sharding import PartitionSpec as P

NZ = 32
NSTEP = 2
NCHEB = 3

coupling = 5.7
time_step = 0.1

LANES = 128
ROWS = 8
F32 = jnp.float32
UPPER = ((0, 1), (0, 2), (1, 2))


def rows_of():
    return lax.broadcasted_iota(jnp.int32, (ROWS, LANES), 0)


def lanes_of():
    return lax.broadcasted_iota(jnp.int32, (ROWS, LANES), 1)


def choose(mask, first, second):
    return jnp.where(jnp.broadcast_to(mask, first.shape), first, second)


def row_roll(values, count):
    count = count % 4
    if count == 0:
        return values
    return pltpu.roll(values, ROWS - 2 * count, axis=values.ndim - 2)


def swap_halves(values):
    axis = values.ndim - 2
    return choose(
        (rows_of() & 1) == 0,
        pltpu.roll(values, ROWS - 1, axis=axis),
        pltpu.roll(values, 1, axis=axis),
    )


def roll_y(values, amount):
    axis = values.ndim - 1
    if amount == 1:
        moved = pltpu.roll(values, LANES - NZ, axis=axis)
        return choose(lanes_of() < LANES - NZ, moved, swap_halves(moved))
    moved = pltpu.roll(values, NZ, axis=axis)
    return choose(lanes_of() >= NZ, moved, swap_halves(moved))


def roll_z(values, amount):
    position = lanes_of() & (NZ - 1)
    axis = values.ndim - 1
    if amount == 1:
        return choose(
            position == NZ - 1,
            pltpu.roll(values, NZ - 1, axis=axis),
            pltpu.roll(values, LANES - 1, axis=axis),
        )
    return choose(
        position == 0,
        pltpu.roll(values, LANES - NZ + 1, axis=axis),
        pltpu.roll(values, 1, axis=axis),
    )


def by_pair(choices):
    row = rows_of()
    low = choices[0] if choices[0] is choices[1] else choose(row < 2, choices[0], choices[1])
    return choose(row < 4, low, choose(row < 6, choices[2], choices[3]))


def product(left, right, left_h=False, right_h=False):
    real = imag = None
    for c in range(3):
        lr, li = (left[0, c], left[1, c]) if left_h else (left[0, :, c], left[1, :, c])
        rr, ri = (right[0, :, c], right[1, :, c]) if right_h else (right[0, c], right[1, c])
        lr, li, rr, ri = lr[:, None], li[:, None], rr[None], ri[None]
        both = lr * rr
        cross = li * ri
        first = lr * ri
        second = li * rr
        re = both + cross if left_h != right_h else both - cross
        if left_h and right_h:
            im = -first - second
        elif left_h:
            im = first - second
        elif right_h:
            im = second - first
        else:
            im = first + second
        real = re if real is None else real + re
        imag = im if imag is None else imag + im
    return jnp.stack([real, imag])


def traceless_part(m):
    parts = [0.5 * (m[0, i, j] - m[0, j, i]) for i, j in UPPER]
    parts += [0.5 * (m[1, i, j] + m[1, j, i]) for i, j in UPPER]
    trace = (m[1, 0, 0] + m[1, 1, 1] + m[1, 2, 2]) * (1.0 / 3.0)
    parts += [m[1, i, i] - trace for i in range(3)]
    return jnp.stack(parts)


def gauge_force(own, plus_t, plus_x, minus_t, minus_x, corner):
    ahead = [plus_t, plus_x, roll_y(own, 1), roll_z(own, 1)]
    behind = [minus_t, minus_x, roll_y(own, -1), roll_z(own, -1)]

    def slanted(arrays, k):
        return by_pair([arrays[(nu - k) % 4] for nu in range(4)])

    diagonal = slanted(behind, 0)
    turned = [
        by_pair([corner, corner, roll_y(plus_t, -1), roll_z(plus_t, -1)]),
        by_pair([corner, corner, roll_y(plus_x, -1), roll_z(plus_x, -1)]),
        roll_y(diagonal, 1),
        roll_z(diagonal, 1),
    ]
    staple = None
    for k in (1, 2, 3):
        up = product(
            product(row_roll(slanted(ahead, k), k), slanted(ahead, 4 - k), right_h=True),
            row_roll(own, k),
            right_h=True,
        )
        low = product(
            product(row_roll(slanted(turned, k), k), slanted(behind, 4 - k), True, True),
            row_roll(diagonal, k),
        )
        staple = up + low if staple is None else staple + up + low
    return (coupling / 3.0) * traceless_part(product(own, staple))


def third_row(two):
    re, im = [], []
    for colour in range(3):
        b, c = (colour + 1) % 3, (colour + 2) % 3
        ar, ai, dr, di = two[0, 0, b], two[1, 0, b], two[0, 1, c], two[1, 1, c]
        er, ei, fr, fi = two[0, 0, c], two[1, 0, c], two[0, 1, b], two[1, 1, b]
        re.append(ar * dr - ai * di - (er * fr - ei * fi))
        im.append(-(ar * di + ai * dr - (er * fi + ei * fr)))
    return jnp.stack([jnp.stack(re), jnp.stack(im)])


def evolve(moment, own):
    a = time_step * moment
    x01, x02, x12 = a[3], a[4], a[5]
    y01, y02, y12 = -a[0], -a[1], -a[2]
    h0, h1, h2 = a[6], a[7], a[8]
    n01 = x01 * x01 + y01 * y01
    n02 = x02 * x02 + y02 * y02
    n12 = x12 * x12 + y12 * y12
    g0 = h0 * h0 + n01 + n02
    g1 = h1 * h1 + n01 + n12
    g2 = h2 * h2 + n02 + n12
    u01 = (h0 + h1) * x01 + (x02 * x12 + y02 * y12)
    v01 = (h0 + h1) * y01 + (y02 * x12 - x02 * y12)
    p02 = x01 * x12 - y01 * y12
    q02 = x01 * y12 + y01 * x12
    u02 = (h0 + h2) * x02 + p02
    v02 = (h0 + h2) * y02 + q02
    u12 = (h1 + h2) * x12 + (x01 * x02 + y01 * y02)
    v12 = (h1 + h2) * y12 + (x01 * y02 - y01 * x02)
    s = 0.5 * (g0 + g1 + g2)
    d = (
        h0 * h1 * h2
        + 2.0 * (p02 * x02 + q02 * y02)
        - h0 * n12
        - h1 * n02
        - h2 * n01
    )
    c0r = 1.0 - d * d * (1.0 / 720.0)
    c0i = d * (s * (1.0 / 120.0) - 1.0 / 6.0)
    c1r = d * (1.0 / 24.0 - s * (1.0 / 360.0))
    c1i = 1.0 + s * (s * (1.0 / 120.0) - 1.0 / 6.0)
    c2r = s * (1.0 / 24.0 - s * (1.0 / 720.0)) - 0.5
    c2i = d * (1.0 / 120.0)
    re = [[None] * 3 for _ in range(3)]
    im = [[None] * 3 for _ in range(3)]
    for i, (h, g) in enumerate(((h0, g0), (h1, g1), (h2, g2))):
        re[i][i] = c0r + c1r * h + c2r * g
        im[i][i] = c0i + c1i * h + c2i * g
    for (i, j), x, y, u, v in (
        ((0, 1), x01, y01, u01, v01),
        ((0, 2), x02, y02, u02, v02),
        ((1, 2), x12, y12, u12, v12),
    ):
        rx = c1r * x + c2r * u
        iy = c1i * y + c2i * v
        ix = c1i * x + c2i * u
        ry = c1r * y + c2r * v
        re[i][j], re[j][i] = rx - iy, rx + iy
        im[i][j], im[j][i] = ix + ry, ix - ry
    e = jnp.stack([jnp.stack([jnp.stack(r) for r in re]), jnp.stack([jnp.stack(r) for r in im])])
    return product(e, own)


def spread(values, pair):
    row = rows_of()
    step = -1 if pair % 2 == 0 else 1
    values = choose((row & 2) == 2 * (pair % 2), values, row_roll(values, step))
    return choose((row & 4) == 4 * (pair // 2), values, row_roll(values, 2))


def matvec(matrix, v, herm=False):
    real = imag = None
    for c in range(3):
        mr, mi = (matrix[0, c], matrix[1, c]) if herm else (matrix[0, :, c], matrix[1, :, c])
        vr, vi = v[0, c][None], v[1, c][None]
        if herm:
            re = mr * vr + mi * vi
            im = mr * vi - mi * vr
        else:
            re = mr * vr - mi * vi
            im = mr * vi + mi * vr
        real = re if real is None else real + re
        imag = im if imag is None else imag + im
    return jnp.stack([real, imag])


def site_links(own):
    return [
        spread(own, 1),
        spread(own, 2),
        spread(roll_y(own, -1), 2),
        spread(own, 3),
        spread(roll_z(own, -1), 3),
    ]


def gather_rows(ref, starts):
    return jnp.concatenate([ref[pl.ds(s, 2), :] for s in starts], axis=0)


def scatter_rows(ref, starts, values):
    for n, s in enumerate(starts):
        ref[pl.ds(s, 2), :] = values[2 * n : 2 * n + 2]


def link_rows(i, j, c):
    return [(((mu * 3 + i) * 3 + j) * 2 + c) * 2 for mu in range(4)]


def vector_rows(tile, a, c, h):
    return [((((4 * tile + n) * 3 + a) * 2 + c) * 2 + h) * 2 for n in range(4)]


def kernel(
    sizes,
    tiles,
    coef,
    links_ref,
    momenta_ref,
    vectors_ref,
    links_out,
    momenta_out,
    vectors_out,
    links_in,
    momenta_in,
    vectors_in,
    two_rows,
    v_in,
    v_done,
    state,
    pair_u,
    got_u,
    got_pair_u,
    send_p,
    pair_p,
    got_p,
    got_pair_p,
    far_u,
    got_far,
    hop_links,
    fields,
    got_fields,
    total,
    partial,
    load_sem,
    send_sem,
    recv_sem,
):
    n_grp, n_ta, n_x = sizes
    ring = n_grp * tiles == n_x and n_x == 4
    grp, ta, x = lax.axis_index("grp"), lax.axis_index("ta"), lax.axis_index("xyz")
    n_t = n_grp * n_ta
    t = grp * n_ta + ta

    def device(dt, dx):
        tt = lax.rem(t + dt + n_t, n_t)
        return (tt // n_ta, lax.rem(tt, n_ta), lax.rem(x + dx + n_x, n_x))

    def beside(dg, dx):
        return (lax.rem(grp + dg, n_grp), ta, lax.rem(x + dx, n_x))

    whole_to = [device(-1, 0), device(0, -1), device(1, 0), device(0, 1)]
    pair_to = [device(1, -1), device(-1, 1)]
    if ring:
        whole_to.append(device(0, 2))
        peers = [device(-1, 0), device(1, 0)] + pair_to
        peers += [beside(dg, dx) for dg in range(n_grp) for dx in range(n_x) if dg or dx]
    else:
        peers = whole_to + pair_to + [beside(1, 0)]
    barrier = pltpu.get_barrier_semaphore()
    for peer in peers:
        pl.semaphore_signal(
            barrier, inc=1, device_id=peer, device_id_type=pl.DeviceIdType.MESH
        )
    loads = [
        pltpu.make_async_copy(links_ref, links_in, load_sem.at[0]),
        pltpu.make_async_copy(vectors_ref, vectors_in, load_sem.at[1]),
        pltpu.make_async_copy(momenta_ref, momenta_in, load_sem.at[2]),
    ]
    for load in loads:
        load.start()
    stores = [
        pltpu.make_async_copy(links_in, links_out, load_sem.at[3]),
        pltpu.make_async_copy(momenta_in, momenta_out, load_sem.at[4]),
        pltpu.make_async_copy(vectors_in, vectors_out, load_sem.at[5]),
    ]

    counter = [0]

    def describe(src, dst, to, send, recv):
        return pltpu.make_async_remote_copy(
            src_ref=src,
            dst_ref=dst,
            send_sem=send_sem.at[send],
            recv_sem=recv_sem.at[recv],
            device_id=to,
            device_id_type=pl.DeviceIdType.MESH,
        )

    def take(count):
        counter[0] += count
        return counter[0] - count

    def copy(src, dst, to):
        n = take(1)
        made = describe(src, dst, to, n, n)
        made.start()
        return made

    pending = []

    loads[0].wait()
    for i in range(3):
        for j in range(3):
            for c in range(2):
                state[0, c, i, j] = gather_rows(links_in, link_rows(i, j, c))
    two_rows[...] = state[0, :, 0:2]
    pair_u[0] = two_rows[:, :, :, 0:2, :]
    pair_u[1] = two_rows[:, :, :, 2:4, :]
    pl.semaphore_wait(barrier, len(peers))

    first = [copy(two_rows, got_u.at[i], whole_to[i]) for i in (1, 3, 0, 2)]
    first += [copy(pair_u.at[i], got_pair_u.at[i], pair_to[i]) for i in range(2)]
    pending += first

    loads[1].wait()
    for h in range(2):
        for tile in range(tiles):
            for c in range(2):
                for a in range(3):
                    v_in[h, tile, c, a] = gather_rows(vectors_in, vector_rows(tile, a, c, h))
    loads[2].wait()
    moment = jnp.stack(
        [gather_rows(momenta_in, link_rows(i, j, 0)) for i, j in UPPER]
        + [gather_rows(momenta_in, link_rows(i, j, 1)) for i, j in UPPER]
        + [gather_rows(momenta_in, link_rows(i, i, 1)) for i in range(3)]
    )
    send_p[0] = moment
    for made in first:
        made.wait_recv()

    if ring:
        own_tile = x // tiles
        home = lax.rem(x, tiles)
        out_send, out_recv = take(2 * tiles), take(n_x)
        moves = []
        for h in range(2):
            for tile in range(tiles):
                target = grp * tiles + tile
                slot = lax.rem(x - target + n_x, n_x)
                here = jnp.logical_and(grp == h, x == target)
                made = describe(
                    v_in.at[h, tile],
                    fields.at[0, slot],
                    (h, ta, target),
                    out_send + h * tiles + tile,
                    out_recv + slot,
                )
                moves.append((here, made))

        @pl.when(own_tile == grp)
        def _():
            fields[0, 0] = v_in[grp, home]

    else:
        give = copy(v_in.at[1 - grp], fields.at[0, tiles : 2 * tiles], beside(1, 0))
        fields[0, 0:tiles] = v_in[grp]
        pending.append(give)

    for i in range(4):
        state[i + 1, :, 0:2] = got_u[i]
        state[i + 1, :, 2] = third_row(got_u[i])
    low, high = got_pair_u[0], got_pair_u[1]
    both = jnp.concatenate([low, high, high, high], axis=3)
    state[5, :, 0:2] = both
    state[5, :, 2] = third_row(both)

    def force():
        return gauge_force(*[state[i] for i in range(6)])

    def send_moment(r, moment):
        send_p[r] = moment
        pair_p[r, 0] = moment[:, 0:2, :]
        pair_p[r, 1] = moment[:, 2:4, :]
        made = [copy(send_p.at[r], got_p.at[r, i], whole_to[i]) for i in (1, 3, 0, 2)]
        made += [copy(pair_p.at[r, i], got_pair_p.at[r, i], pair_to[i]) for i in range(2)]
        return made

    def send_fields(r):
        return [
            copy(fields.at[r], got_fields.at[r, 0], whole_to[1]),
            copy(fields.at[r], got_fields.at[r, 1], whole_to[3]),
        ]

    halo = None
    entries = [(c, i, j) for c in range(2) for i in range(3) for j in range(3)]

    def far_rows(n):
        return [2 * (len(entries) * d + n) for d in range(3)]

    moment = send_p[0] - (0.5 * time_step) * force()
    for r in range(NSTEP):
        made = send_moment(r, moment)
        pending += made
        if r == 0 and not ring:
            give.wait_recv()
            halo = send_fields(0)
            pending += halo
        state[0] = evolve(moment, state[0])
        if ring and r + 1 == NSTEP:
            for n, (c, i, j) in enumerate(entries):
                scatter_rows(far_u, far_rows(n), state[0, c, i, j][2:])
            far_u[pl.ds(6 * len(entries), 4), :] = jnp.zeros((4, LANES), F32)
            far = copy(far_u, got_far, whole_to[4])
            pending.append(far)
        for i, one in ((0, made[2]), (2, made[3])):
            one.wait_recv()
            state[i + 1] = evolve(got_p[r, i], state[i + 1])
        for one in made[4:]:
            one.wait_recv()
        low, high = got_pair_p[r, 0], got_pair_p[r, 1]
        state[5] = evolve(jnp.concatenate([low, high, high, high], axis=1), state[5])
        made[0].wait_recv()
        made[1].wait_recv()
        if ring and r == 0:
            for here, one in moves:
                pl.when(jnp.logical_not(here))(one.start)
        for i in (1, 3):
            state[i + 1] = evolve(got_p[r, i], state[i + 1])
        if r + 1 < NSTEP:
            moment = moment - time_step * force()

    def finish_momenta():
        done = moment - (0.5 * time_step) * force()
        zero = jnp.zeros_like(done[0])
        for n, (i, j) in enumerate(UPPER):
            scatter_rows(momenta_in, link_rows(i, j, 0), done[n])
            scatter_rows(momenta_in, link_rows(j, i, 0), -done[n])
            scatter_rows(momenta_in, link_rows(i, j, 1), done[n + 3])
            scatter_rows(momenta_in, link_rows(j, i, 1), done[n + 3])
        for i in range(3):
            scatter_rows(momenta_in, link_rows(i, i, 0), zero)
            scatter_rows(momenta_in, link_rows(i, i, 1), done[6 + i])
        stores[1].start()

    def finish_links():
        for i in range(3):
            for j in range(3):
                for c in range(2):
                    scatter_rows(links_in, link_rows(i, j, c), state[0, c, i, j])
        stores[0].start()

    def step(k, g, acc):
        acc = acc * (-1.0 / 6.0)
        if k == 0:
            fields[1, g] = acc
            total[g] = coef[0] * fields[0, g] + coef[1] * acc
        else:
            following = 2.0 * acc - fields[k - 1, g]
            if k + 1 < NCHEB:
                fields[k + 1, g] = following
            total[g] = total[g] + coef[k + 1] * following

    def hop_local(k, g, at):
        v = fields[k, g]
        acc = matvec(hop_links[at, 1], roll_y(v, 1))
        acc = acc + matvec(hop_links[at, 2], roll_y(v, -1), True)
        acc = acc + matvec(hop_links[at, 3], roll_z(v, 1))
        return acc + matvec(hop_links[at, 4], roll_z(v, -1), True)

    def store_links(at, slot):
        for n, matrix in enumerate(site_links(state[slot])):
            hop_links[at, n] = matrix

    if ring:
        for at, slot in ((0, 0), (1, 2), (3, 4)):
            store_links(at, slot)
        for slot in range(n_x):
            waiter = describe(v_in.at[0, 0], fields.at[0, slot], beside(1, 0), 0, out_recv + slot)
            if slot:
                waiter.wait_recv()
            else:
                pl.when(own_tile != grp)(waiter.wait_recv)

        def hop(k, g):
            after, before = lax.rem(g + 1, n_x), lax.rem(g + n_x - 1, n_x)
            acc = hop_local(k, g, g)
            acc = acc + matvec(hop_links[g, 0], fields[k, after])
            acc = acc + matvec(hop_links[before, 0], fields[k, before], True)
            step(k, g, acc)

        pl.loop(0, 2)(functools.partial(hop, 0))
        far.wait_recv()
        for n, (c, i, j) in enumerate(entries):
            starts = far_rows(n)
            state[6, c, i, j] = gather_rows(got_far, starts[:1] + starts)
        store_links(2, 6)
        pl.loop(2, n_x)(functools.partial(hop, 0))
        for k in range(1, NCHEB - 1):
            pl.loop(0, n_x)(functools.partial(hop, k))

        back_send, back_recv = take(n_x), take(2 * tiles)
        backs = []
        for g in (2, 1, 3, 0):
            hop(NCHEB - 1, g)
            made = describe(
                total.at[g],
                v_done.at[grp, home],
                (own_tile, ta, lax.rem(x + g, n_x)),
                back_send + g,
                back_recv + grp * tiles + home,
            )
            backs.append((g, made))
            if g:
                made.start()
            else:
                pl.when(own_tile != grp)(made.start)

        @pl.when(own_tile == grp)
        def _():
            v_done[grp, home] = total[0]

        finish_links()
        finish_momenta()
        for h in range(2):
            for tile in range(tiles):
                here, _ = moves[h * tiles + tile]
                waiter = describe(
                    total.at[0],
                    v_done.at[h, tile],
                    beside(1, 0),
                    0,
                    back_recv + h * tiles + tile,
                )
                pl.when(jnp.logical_not(here))(waiter.wait_recv)
        for here, made in moves:
            pl.when(jnp.logical_not(here))(made.wait_send)
        for g, made in backs:
            if g:
                made.wait_send()
            else:
                pl.when(own_tile != grp)(made.wait_send)
    else:
        store_links(0, 0)
        hop_links[1, 0] = spread(state[4], 1)
        finish_links()
        for k in range(NCHEB):
            if k:
                halo = send_fields(k)
                pending += halo
            if k == 1:
                finish_momenta()

            @pl.loop(0, 2 * tiles)
            def _(g):
                partial[g] = hop_local(k, g, 0)

            for one in halo:
                one.wait_recv()

            @pl.loop(0, 2 * tiles)
            def _(g):
                acc = partial[g] + matvec(hop_links[0, 0], got_fields[k, 0, g])
                acc = acc + matvec(hop_links[1, 0], got_fields[k, 1, g], True)
                step(k, g, acc)

        back = copy(total.at[tiles : 2 * tiles], v_done.at[grp], beside(1, 0))
        v_done[grp] = total[0:tiles]
        back.wait_recv()
        pending.append(back)

    for h in range(2):
        for tile in range(tiles):
            for c in range(2):
                for a in range(3):
                    scatter_rows(vectors_in, vector_rows(tile, a, c, h), v_done[h, tile, c, a])
    stores[2].start()
    for one in pending:
        one.wait_send()
    for one in stores:
        one.wait()


def leave(*refs):
    ins, outs, held, sem = refs[0:3], refs[3:6], refs[6:9], refs[9]
    loads = [pltpu.make_async_copy(ins[n], held[n], sem.at[n]) for n in range(3)]
    stores = [pltpu.make_async_copy(held[n], outs[n], sem.at[n + 3]) for n in range(3)]
    for one in loads:
        one.start()
    for load, store in zip(loads, stores):
        load.wait()
        store.start()
    for one in stores:
        one.wait()


def body(sizes, links, momenta, vectors, coefficients):
    tiles = vectors.shape[0] * 2 // ROWS
    groups = 2 * tiles
    copies = 2 * (groups + 4) + 7 + 7 * NSTEP + 2 * NCHEB + 2
    hbm = pl.BlockSpec(memory_space=pltpu.HBM)
    tile = (ROWS, LANES)
    flat_links = (links.size // LANES, LANES)
    flat_vectors = (vectors.size // LANES, LANES)
    new_links, new_momenta, filtered = pl.pallas_call(
        functools.partial(kernel, sizes, tiles),
        out_shape=(
            jax.ShapeDtypeStruct(flat_links, F32),
            jax.ShapeDtypeStruct(flat_links, F32),
            jax.ShapeDtypeStruct(flat_vectors, F32),
        ),
        in_specs=[pl.BlockSpec(memory_space=pltpu.SMEM)] + [hbm] * 3,
        out_specs=(hbm,) * 3,
        scratch_shapes=[
            pltpu.VMEM(flat_links, F32),
            pltpu.VMEM(flat_links, F32),
            pltpu.VMEM(flat_vectors, F32),
            pltpu.VMEM((2, 2, 3) + tile, F32),
            pltpu.VMEM((2, tiles, 2, 3) + tile, F32),
            pltpu.VMEM((2, tiles, 2, 3) + tile, F32),
            pltpu.VMEM((7, 2, 3, 3) + tile, F32),
            pltpu.VMEM((2, 2, 2, 3, 2, LANES), F32),
            pltpu.VMEM((4, 2, 2, 3) + tile, F32),
            pltpu.VMEM((2, 2, 2, 3, 2, LANES), F32),
            pltpu.VMEM((NSTEP, 9) + tile, F32),
            pltpu.VMEM((NSTEP, 2, 9, 2, LANES), F32),
            pltpu.VMEM((NSTEP, 4, 9) + tile, F32),
            pltpu.VMEM((NSTEP, 2, 9, 2, LANES), F32),
            pltpu.VMEM((112, LANES), F32),
            pltpu.VMEM((112, LANES), F32),
            pltpu.VMEM((4, 5, 2, 3, 3) + tile, F32),
            pltpu.VMEM((NCHEB, groups, 2, 3) + tile, F32),
            pltpu.VMEM((NCHEB, 2, groups, 2, 3) + tile, F32),
            pltpu.VMEM((groups, 2, 3) + tile, F32),
            pltpu.VMEM((groups, 2, 3) + tile, F32),
            pltpu.SemaphoreType.DMA((6,)),
            pltpu.SemaphoreType.DMA((copies,)),
            pltpu.SemaphoreType.DMA((copies,)),
        ],
        compiler_params=pltpu.CompilerParams(
            collective_id=0, has_side_effects=True, vmem_limit_bytes=60 * 1024 * 1024
        ),
    )(
        coefficients,
        links.reshape(flat_links),
        momenta.reshape(flat_links),
        vectors.reshape(flat_vectors),
    )
    new_links, new_momenta, filtered = pl.pallas_call(
        leave,
        out_shape=(
            jax.ShapeDtypeStruct(flat_links, F32),
            jax.ShapeDtypeStruct(flat_links, F32),
            jax.ShapeDtypeStruct(flat_vectors, F32),
        ),
        in_specs=[hbm] * 3,
        out_specs=(hbm,) * 3,
        scratch_shapes=[
            pltpu.VMEM(flat_links, F32),
            pltpu.VMEM(flat_links, F32),
            pltpu.VMEM(flat_vectors, F32),
            pltpu.SemaphoreType.DMA((6,)),
        ],
        compiler_params=pltpu.CompilerParams(vmem_limit_bytes=60 * 1024 * 1024),
    )(new_links, new_momenta, filtered)
    return (
        new_links.reshape(links.shape),
        new_momenta.reshape(momenta.shape),
        filtered.reshape(vectors.shape),
    )


def solution(mesh):
    sizes = (mesh.shape["grp"], mesh.shape["ta"], mesh.shape["xyz"])
    link_spec = P(None, None, None, None, ("grp", "ta"), "xyz", None)
    vector_spec = P("grp", None, None, None, "ta", "xyz", None)
    return jax.shard_map(
        functools.partial(body, sizes),
        mesh=mesh,
        in_specs=(link_spec, link_spec, vector_spec, P()),
        out_specs=(link_spec, link_spec, vector_spec),
        check_vma=False,
    )
```
